32 devices in a mesh: samp: 8 (over z, x), chan: 4 (over y, core).
Axes of the slice: x: 2, y: 2, z: 4, core: 2. Of those that a mesh axis runs over, the one named last changes fastest.
Arguments:
- loads: float32 [256, 24576], P('chan', 'samp')
- coords: float32 [6, 24576], P(None, 'samp'), may hold values from -6 to 6
- coreg_factor: float32 [256, 256], P('chan'), may hold values from -0.375 to 0.375
- noise: float32 [256], P('chan'), may hold values from 0.1 to 1
- run_perm: int32 [24576], P('samp'), may hold values from 0 to 24575, as said below
- block_nbrs: int32 [192, 12], P('samp'), may hold values from 0 to 191, as said below
- nbr_count: int32 [192], P('samp'), may hold values from 1 to 12, as said below
Outputs:
- solution: float32 [256, 24576], P('chan', 'samp')
- residual: float32 [256, 24576], P('chan', 'samp')
The draws below stay inside these ranges and needn't reach their ends.
Inputs may be any that keep to these rules, and one draw needn't show every extreme that they name: `block_nbrs`: the blocks are cut into clusters of consecutive blocks, each of 1 to 12 blocks. Row b lists the blocks of b's cluster in increasing order in its first nbr_count[b] entries; its other entries hold b itself. `nbr_count`: the size of block b's cluster; some block's cluster has 12 blocks. `run_perm`: within each aligned range of 3072 positions (the runs of one samp device), a permutation of that range.
All inputs are finite; a program needn't handle non-finite values.
Results may differ from the reference program's by a relative error of at most 0.0035.
Values may be sent and summed in bfloat16 or wider, within the bound.
A program may use at most 64 MiB of HBM per device.

```python
import math
import jax
import jax.numpy as jnp
from jax import lax

CH = 256
DIM = 6
BS = 128
MAXC = 12
ITERS = 2
BLK_DEV = 24
NBLK = 192
RUNS = 24576


def draw_loads(key, part):
    key_vals, key_rows, key_cols = jax.random.split(key, 3)
    position = jnp.arange(RUNS).astype(jnp.float32) / RUNS
    row_scale = jnp.exp(jax.random.uniform(key_rows, (RUNS,), jnp.float32, -1.2, 1.2))
    col_scale = jnp.exp(jax.random.uniform(key_cols, (CH,), jnp.float32, -1.2, 1.2))
    values = jax.random.normal(key_vals, (CH, RUNS), jnp.float32)
    trend = 0.6 + 1.2 * position
    return (values * col_scale[:, None] * (row_scale * trend)[None, :]).astype(jnp.float32)


def draw_run_perm(key, part):
    per_device = BLK_DEV * BS
    device_count = RUNS // per_device
    keys = jax.random.split(jax.random.fold_in(key, 5), device_count)
    perms = jax.vmap(lambda one_key: jax.random.permutation(one_key, per_device))(keys)
    shifted = perms + (jnp.arange(device_count) * per_device)[:, None]
    return shifted.reshape(-1).astype(jnp.int32)


def cluster_pattern(key):
    base = jax.random.fold_in(key, 11)
    key_level, key_len, key_phase = jax.random.split(base, 3)
    clusters = NBLK
    levels = jax.random.randint(key_level, (clusters // 16 + 1,), 1, 5)
    caps = jnp.maximum(1, MAXC * levels // 4)
    cap_each = jnp.repeat(caps, 16)[:clusters]
    raw = jax.random.randint(key_len, (clusters,), 0, 1 << 20)
    drawn = raw % cap_each + 1
    phase = jax.random.randint(key_phase, (), 0, 4)
    order = jnp.arange(clusters)
    drawn = jnp.where(order % 8 == phase, MAXC, drawn)
    ends = jnp.cumsum(drawn)
    blocks = jnp.arange(NBLK)
    cluster_of = jnp.sum((ends[None, :] <= blocks[:, None]).astype(jnp.int32), axis=1)
    begins = jnp.where(cluster_of > 0, ends[jnp.maximum(cluster_of - 1, 0)], 0)
    finish = jnp.minimum(ends[cluster_of], NBLK)
    counts = finish - begins
    slots = jnp.arange(MAXC)
    listed = jnp.where(slots[None, :] < counts[:, None], begins[:, None] + slots[None, :], blocks[:, None])
    return (listed.astype(jnp.int32), counts.astype(jnp.int32))


def draw_block_nbrs(key, part):
    return cluster_pattern(key)[0]


def draw_nbr_count(key, part):
    return cluster_pattern(key)[1]


def level_of(key, shape, shards, smallest, top_value):
    factor_of, own = 1.0, jax.random.fold_in(key, 6)
    for dim, parts in shards:
        draws = jnp.exp(jax.random.uniform(jax.random.fold_in(own, dim), (parts,), jnp.float32, smallest / len(shards), top_value / len(shards)))
        factor_of = factor_of * jnp.repeat(draws, shape[dim] // parts).reshape([-1 if axis == dim else 1 for axis in range(len(shape))])
    return factor_of


def centred(key, extent, scale, bound, cuts=(), kind=jnp.bfloat16):
    loudness = level_of(key, extent, cuts, -0.22, 0.18) if cuts else 1.0
    values = jax.random.normal(key, extent, jnp.float32) * scale * loudness
    return jnp.minimum(jnp.maximum(values, -bound), bound).astype(kind)


def setup_inputs(seed: int = 0) -> dict:
    streams_of = jax.random.split(jax.random.key(seed), 8)
    loads = draw_loads(jax.random.fold_in(streams_of[7], 71), 0)
    coords = centred(streams_of[1], (DIM, RUNS), 1.0, 6.0, ((1, 8),), jnp.float32)
    coreg_factor = centred(streams_of[2], (CH, CH), CH ** -0.5, 0.375, ((0, 4),), jnp.float32)
    noise = jnp.clip(jnp.exp(math.log(1.0) - 2.3025851 * jax.random.uniform(streams_of[3], (CH,), jnp.float32) ** level_of(streams_of[3], (CH,), ((0, 4),), -0.2, 0.2)), 0.1, 1.0)
    run_perm = draw_run_perm(jax.random.fold_in(streams_of[7], 71), 0)
    block_nbrs = draw_block_nbrs(jax.random.fold_in(streams_of[7], 71), 0)
    nbr_count = draw_nbr_count(jax.random.fold_in(streams_of[7], 71), 0)
    return {"loads": loads, "coords": coords, "coreg_factor": coreg_factor, "noise": noise, "run_perm": run_perm, "block_nbrs": block_nbrs, "nbr_count": nbr_count}


SUPPORT = 5.0
AMPLITUDE = 0.05

def wendland(squared):
    radius_frac = jnp.sqrt(squared) / SUPPORT
    remain = jnp.maximum(1.0 - radius_frac, 0.0)
    cubed = remain * remain * remain
    return cubed * cubed * (6.0 * radius_frac + 1.0)

def apply_operator(operand, coreg, coord_blocks, block_nbrs, nbr_count, noise):
    rounded = operand.astype(jnp.bfloat16)
    mixed = jnp.dot(coreg, rounded.astype(jnp.float32), precision=lax.Precision.HIGHEST)
    mixed_b = mixed.astype(jnp.bfloat16)
    value_blocks = mixed_b.reshape(CH, NBLK, BS)
    own_coords = coord_blocks

    def slot_step(slot_index, summed):
        partner_ids = lax.dynamic_index_in_dim(block_nbrs, slot_index, 1, keepdims=False)
        live_mask = (slot_index < nbr_count).astype(jnp.float32)
        partner = jnp.take(coord_blocks, partner_ids, axis=1)
        squared = jnp.zeros((NBLK, BS, BS), jnp.float32)
        for component in range(DIM):
            difference = own_coords[component][:, :, None] - partner[component][:, None, :]
            squared = squared + difference * difference
        kernel_tile = (wendland(squared) * live_mask[:, None, None]).astype(jnp.bfloat16)
        partner_vals = jnp.take(value_blocks, partner_ids, axis=1)
        return summed + jnp.einsum('bim,cbm->cbi', kernel_tile.astype(jnp.float32), partner_vals.astype(jnp.float32))
    summed = lax.fori_loop(0, MAXC, slot_step, jnp.zeros((CH, NBLK, BS), jnp.float32))
    return AMPLITUDE * summed.reshape(CH, RUNS) + noise[:, None] * operand

def reference(loads, coords, coreg_factor, noise, run_perm, block_nbrs, nbr_count):
    coreg = jnp.dot(coreg_factor, coreg_factor.T, precision=lax.Precision.HIGHEST)
    sorted_coords = jnp.take(coords, run_perm, axis=1)
    sorted_loads = jnp.take(loads, run_perm, axis=1)
    coord_blocks = sorted_coords.reshape(DIM, NBLK, BS)
    iterate = jnp.zeros_like(sorted_loads)
    remainder = sorted_loads
    direction = sorted_loads
    norm_now = jnp.sum(remainder * remainder)
    for iteration in range(ITERS):
        mapped = apply_operator(direction, coreg, coord_blocks, block_nbrs, nbr_count, noise)
        step_size = norm_now / jnp.sum(direction * mapped)
        iterate = iterate + step_size * direction
        remainder = remainder - step_size * mapped
        if iteration + 1 < ITERS:
            norm_next = jnp.sum(remainder * remainder)
            direction = remainder + norm_next / norm_now * direction
            norm_now = norm_next
    solution = jnp.zeros((CH, RUNS), jnp.float32).at[:, run_perm].set(iterate)
    residual = jnp.zeros((CH, RUNS), jnp.float32).at[:, run_perm].set(remainder)
    return (solution, residual)
```

```python
import functools

import jax
import jax.numpy as jnp
from jax import lax
from jax.experimental import pallas as pl
from jax.experimental.pallas import tpu as pltpu
from jax.sharding import PartitionSpec as P

SUPPORT = 5.0
AMPLITUDE = 0.05
LANES = 128
CHUNKS = 4
MESH = pl.DeviceIdType.MESH
F32 = jnp.float32
BF16 = jnp.bfloat16


def lane_tile(index):
    return pl.ds(pl.multiple_of(index * LANES, LANES), LANES)


def permute_tiles(source, order, target, begin, end):
    rows, columns = source.shape

    def step(tile, carry):
        index = order[pl.ds(tile, 1), :]
        lane = jnp.broadcast_to(index % LANES, (rows, LANES))
        origin = jnp.broadcast_to(index // LANES, (rows, LANES))
        result = jnp.zeros((rows, LANES), F32)
        for part in range(columns // LANES):
            picked = jnp.take_along_axis(
                source[:, part * LANES : (part + 1) * LANES], lane, axis=1, mode="promise_in_bounds"
            )
            result = jnp.where(origin == part, picked, result)
        target[:, lane_tile(tile)] = result
        return carry

    lax.fori_loop(begin, end, step, 0)


def pieces(value):
    high = value.astype(BF16).astype(F32)
    rest = value - high
    middle = rest.astype(BF16).astype(F32)
    return high, middle, (rest - middle).astype(BF16).astype(F32)


def fold(value):
    total = value[0:8]
    for row in range(8, value.shape[0], 8):
        total = total + value[row : row + 8]
    return total


def whole_sum(value):
    return jnp.sum(jnp.sum(value, axis=0, keepdims=True), axis=1, keepdims=True)


def sorter(blocks, loads, coords, perm, sorted_loads, sorted_coords, order, coords_in):
    order[...] = perm[...] - lax.axis_index("samp") * loads.shape[1]
    coords_in[...] = jnp.zeros_like(coords_in)
    coords_in[0 : coords.shape[0], :] = coords[...] * (1.0 / SUPPORT)
    permute_tiles(coords_in, order, sorted_coords, 0, blocks)
    permute_tiles(loads, order, sorted_loads, 0, blocks)


def unsorter(blocks, sorted_sol, sorted_res, inverse, sol, res, order):
    order[...] = inverse[...].astype(jnp.int32)
    permute_tiles(sorted_sol, order, sol, 0, blocks)
    permute_tiles(sorted_res, order, res, 0, blocks)


def solver(
    samp_count, blocks, slots,
    sorted_loads, sorted_coords, factor, noise, perm, counts, first_block,
    sol, res, inverse,
    inv_sum, coords_ext, own_terms, ext_terms, tiles,
    factors, coreg, direction, image, gathered, values_first, values_second,
    red_chan, red_samp,
    fac_send, fac_recv, gat_send, gat_recv, halo_send, halo_recv,
    rc_send, rc_recv, rs_send, rs_recv,
):
    rows, runs = sorted_loads.shape
    halo = (slots - 1) * LANES
    extent = runs + 2 * halo
    edge = slots - 1
    widened = blocks + 2 * edge
    values = (values_first, values_second)
    chunk = runs // CHUNKS
    samp = lax.axis_index("samp")
    chan = lax.axis_index("chan")
    core_peer = chan + 1 - 2 * (chan % 2)
    far_peer = (chan + 2) % 4
    chan_peers = (core_peer, far_peer, 3 - chan)

    barrier = pltpu.get_barrier_semaphore()
    for peer in chan_peers:
        pl.semaphore_signal(barrier, inc=1, device_id={"chan": peer}, device_id_type=MESH)

    def greet(hop, carry):
        pl.semaphore_signal(
            barrier, inc=1, device_id={"samp": (samp + hop) % samp_count}, device_id_type=MESH
        )
        return carry

    lax.fori_loop(1, samp_count, greet, 0)

    coords_ext[:, halo : halo + runs] = sorted_coords[...]

    @pl.when(samp == 0)
    def _():
        coords_ext[:, 0:halo] = jnp.zeros((8, halo), F32)
        for turn in range(2):
            values[turn][0:edge] = jnp.zeros((edge, rows, LANES), BF16)

    @pl.when(samp == samp_count - 1)
    def _():
        coords_ext[:, extent - halo : extent] = jnp.zeros((8, halo), F32)
        for turn in range(2):
            values[turn][widened - edge : widened] = jnp.zeros((edge, rows, LANES), BF16)

    factors[chan] = factor[...]
    pl.semaphore_wait(barrier, 3 + samp_count - 1)

    def halo_copies(regions, turn):
        own_low, own_high, low, high = regions
        to_low = pltpu.make_async_remote_copy(
            src_ref=own_low,
            dst_ref=high,
            send_sem=halo_send.at[turn, 0],
            recv_sem=halo_recv.at[turn, 0],
            device_id={"samp": (samp + samp_count - 1) % samp_count},
            device_id_type=MESH,
        )
        to_high = pltpu.make_async_remote_copy(
            src_ref=own_high,
            dst_ref=low,
            send_sem=halo_send.at[turn, 1],
            recv_sem=halo_recv.at[turn, 1],
            device_id={"samp": (samp + 1) % samp_count},
            device_id_type=MESH,
        )
        return to_low, to_high

    def halo_start_low(copies):
        @pl.when(samp > 0)
        def _():
            copies[0].start()

    def halo_start_high(copies):
        @pl.when(samp < samp_count - 1)
        def _():
            copies[1].start()

    def halo_wait(copies):
        @pl.when(samp > 0)
        def _():
            copies[0].wait_send()
            copies[1].wait_recv()

        @pl.when(samp < samp_count - 1)
        def _():
            copies[1].wait_send()
            copies[0].wait_recv()

    coord_copies = halo_copies(
        [coords_ext.at[:, pl.ds(first, halo)] for first in (halo, runs, 0, extent - halo)], 0
    )
    halo_start_low(coord_copies)
    halo_start_high(coord_copies)

    factor_copies = []
    for relation, peer in enumerate(chan_peers):
        factor_copies.append(
            pltpu.make_async_remote_copy(
                src_ref=factors.at[chan],
                dst_ref=factors.at[chan],
                send_sem=fac_send.at[relation],
                recv_sem=fac_recv.at[relation],
                device_id={"chan": peer},
                device_id_type=MESH,
            )
        )
        factor_copies[-1].start()

    def gather_copy(turn, kind, part, owner, peer):
        place = gathered.at[turn, owner, :, pl.ds(part * chunk, chunk)]
        return pltpu.make_async_remote_copy(
            src_ref=place,
            dst_ref=place,
            send_sem=gat_send.at[turn, kind, part],
            recv_sem=gat_recv.at[turn, kind, part],
            device_id={"chan": peer},
            device_id_type=MESH,
        )

    def gather_start(turn, part):
        gather_copy(turn, 1, part, chan, far_peer).start()
        gather_copy(turn, 0, part, chan, core_peer).start()

    def gather_forward(turn, part):
        gather_copy(turn, 1, part, far_peer, far_peer).wait_recv()
        gather_copy(turn, 2, part, far_peer, core_peer).start()

    def gather_finish(turn):
        for part in range(CHUNKS):
            gather_copy(turn, 0, part, chan, core_peer).wait_send()
            gather_copy(turn, 1, part, chan, far_peer).wait_send()
            gather_copy(turn, 2, part, far_peer, core_peer).wait_send()
            gather_copy(turn, 0, part, core_peer, core_peer).wait_recv()
            gather_copy(turn, 2, part, 3 - chan, core_peer).wait_recv()

    per_chunk = blocks // CHUNKS
    for part in range(CHUNKS):
        columns = pl.ds(part * chunk, chunk)
        gathered[0, chan, :, columns] = sorted_loads[:, columns].astype(BF16)
        gather_start(0, part)

    row_id = lax.broadcasted_iota(jnp.int32, (8, LANES), 0)

    def own_step(tile, carry):
        point = sorted_coords[:, lane_tile(tile)]
        norm = jnp.sum(point * point, axis=0, keepdims=True)
        terms = jnp.where(row_id == 6, 1.0, jnp.where(row_id == 7, norm, -2.0 * point))
        high, middle, low = pieces(terms)
        stacked = jnp.concatenate(
            [high, middle, high, middle, low, high, jnp.zeros((LANES - 48, LANES), F32)], axis=0
        )
        own_terms[:, lane_tile(tile)] = stacked.astype(BF16)
        return carry

    lax.fori_loop(0, blocks, own_step, 0)
    halo_wait(coord_copies)

    def ext_step(tile, carry):
        point = coords_ext[:, lane_tile(tile)]
        norm = jnp.sum(point * point, axis=0, keepdims=True)
        terms = jnp.where(row_id == 6, norm, jnp.where(row_id == 7, 1.0, point))
        high, middle, low = pieces(terms)
        stacked = jnp.concatenate(
            [high, high, middle, middle, high, low, jnp.zeros((LANES - 48, LANES), F32)], axis=0
        )
        ext_terms[tile] = stacked.T.astype(BF16)
        return carry

    lax.fori_loop(0, extent // LANES, ext_step, 0)

    def window_start(block):
        return first_block[block]

    def tile_step(block, carry):
        start = window_start(block)
        count = counts[pl.ds(block, 1), :]
        own = own_terms[:, lane_tile(block)]
        for slot in range(slots):
            partner = ext_terms[start + slot]
            squared = jnp.dot(partner, own, preferred_element_type=F32)
            squared = jnp.maximum(squared, 1e-20)
            radius = squared * lax.rsqrt(squared)
            live = jnp.where(count > slot, 1.0, 0.0)
            remain = jnp.maximum(live - radius, 0.0)
            cubed = remain * remain * remain
            tile = cubed * cubed * (6.0 * radius + 1.0)
            tiles[block, slot * LANES : (slot + 1) * LANES, :] = tile.astype(BF16)
        return carry

    first_part = (blocks * 5) // 8
    lax.fori_loop(0, first_part, tile_step, 0)
    for part in range(CHUNKS):
        gather_forward(0, part)
    lax.fori_loop(first_part, blocks, tile_step, 0)

    for copy in factor_copies:
        copy.wait()
    coreg_rows = lax.dot_general(
        factor[...],
        factors[...].reshape(4 * rows, factor.shape[1]),
        (((1,), (1,)), ((), ())),
        precision=lax.Precision.HIGHEST,
        preferred_element_type=F32,
    )
    for number, piece in enumerate(pieces(coreg_rows)):
        coreg[number * rows : (number + 1) * rows, :] = piece.astype(BF16)

    def mix(turn, begin, end):
        weights = coreg[...]
        while begin < end:
            width = min(2 * LANES, end - begin)
            operand = gathered[turn, :, :, begin : begin + width].reshape(4 * rows, width)
            product = jnp.dot(weights, operand, preferred_element_type=F32)
            mixed = product[0:rows] + product[rows : 2 * rows] + product[2 * rows : 3 * rows]
            for part in range(width // LANES):
                values[turn][edge + begin // LANES + part] = mixed[
                    :, part * LANES : (part + 1) * LANES
                ].astype(BF16)
            begin += width

    def exchange(turn):
        copies = halo_copies(
            [
                values[turn].at[pl.ds(first, edge)]
                for first in (edge, blocks, 0, widened - edge)
            ],
            turn + 1,
        )
        mix(turn, 0, halo)
        halo_start_low(copies)
        if runs - halo >= halo:
            mix(turn, runs - halo, runs)
            halo_start_high(copies)
            mix(turn, halo, runs - halo)
        halo_wait(copies)

    noise_wide = jnp.broadcast_to(noise[...], (rows, LANES))
    nothing = jnp.zeros((rows, LANES), F32)

    def apply_block(turn, block, operand):
        start = window_start(block)
        partner = jnp.concatenate([values[turn][start + slot] for slot in range(slots)], axis=1)
        summed = jnp.dot(partner, tiles[block], preferred_element_type=F32)
        return AMPLITUDE * summed + noise_wide * operand

    def reduce_chan_copy(turn, relation, owner, peer):
        return pltpu.make_async_remote_copy(
            src_ref=red_chan.at[turn, owner],
            dst_ref=red_chan.at[turn, owner],
            send_sem=rc_send.at[turn, relation],
            recv_sem=rc_recv.at[turn, relation],
            device_id={"chan": peer},
            device_id_type=MESH,
        )

    def reduce_begin(turn, parts):
        for number, part in enumerate(parts):
            red_chan[turn, chan, number * 8 : (number + 1) * 8, :] = fold(part)
        for number in range(len(parts), 3):
            red_chan[turn, chan, number * 8 : (number + 1) * 8, :] = jnp.zeros((8, LANES), F32)
        for relation, peer in enumerate(chan_peers):
            reduce_chan_copy(turn, relation, chan, peer).start()

    def reduce_samp_copy(turn, hop, owner):
        return pltpu.make_async_remote_copy(
            src_ref=red_samp.at[turn, owner],
            dst_ref=red_samp.at[turn, owner],
            send_sem=rs_send.at[turn, hop],
            recv_sem=rs_recv.at[turn, owner],
            device_id={"samp": (samp + hop) % samp_count},
            device_id_type=MESH,
        )

    def reduce_middle(turn):
        for relation, peer in enumerate(chan_peers):
            reduce_chan_copy(turn, relation, chan, peer).wait_send()
            reduce_chan_copy(turn, relation, peer, peer).wait_recv()
        total = red_chan[turn, 0] + red_chan[turn, 1] + red_chan[turn, 2] + red_chan[turn, 3]
        red_samp[turn, samp] = total

        def send(hop, carry):
            reduce_samp_copy(turn, hop, samp).start()
            return carry

        lax.fori_loop(1, samp_count, send, 0)

    def reduce_end(turn):
        def wait(hop, carry):
            reduce_samp_copy(turn, hop, samp).wait_send()
            reduce_samp_copy(turn, hop, (samp + hop) % samp_count).wait_recv()
            return carry

        lax.fori_loop(1, samp_count, wait, 0)

        def add(index, total):
            return total + red_samp[turn, index]

        total = lax.fori_loop(0, samp_count, add, jnp.zeros((24, LANES), F32))
        return [whole_sum(total[number * 8 : (number + 1) * 8]) for number in range(3)]

    gather_finish(0)
    exchange(0)

    def first_apply(block, carry):
        norm, dot, square = carry
        operand = sorted_loads[:, lane_tile(block)]
        mapped = apply_block(0, block, operand)
        image[:, lane_tile(block)] = mapped
        return norm + operand * operand, dot + operand * mapped, square + mapped * mapped

    sums = lax.fori_loop(0, blocks, first_apply, (nothing, nothing, nothing))
    reduce_begin(0, sums)
    reduce_middle(0)
    norm_now, dot, square = reduce_end(0)
    first_step = norm_now / dot
    norm_next = jnp.maximum(
        norm_now - 2.0 * first_step * dot + first_step * first_step * square, 0.0
    )
    ratio = norm_next / norm_now

    norm_sum = nothing
    for part in range(CHUNKS):
        for tile in range(part * per_chunk, (part + 1) * per_chunk):
            columns = slice(tile * LANES, (tile + 1) * LANES)
            operand = sorted_loads[:, columns]
            remainder = operand - first_step * image[:, columns]
            norm_sum = norm_sum + remainder * remainder
            step = remainder + ratio * operand
            direction[:, columns] = step
            gathered[1, chan, :, columns] = step.astype(BF16)
        gather_start(1, part)

    inv_sum[...] = jnp.zeros_like(inv_sum)
    lane_id = lax.broadcasted_iota(jnp.int32, (LANES, LANES), 1).astype(F32)
    sub_id = lax.broadcasted_iota(jnp.int32, (LANES, LANES), 0).astype(F32)

    def inverse_step(tile, carry):
        index = jnp.broadcast_to(perm[pl.ds(tile, 1), :].astype(F32), (LANES, LANES))
        target = index.T - lane_id
        position = sub_id + (tile * LANES).astype(F32)
        for part in range(blocks):
            hit = jnp.where(target == float(part * LANES), position, 0.0)
            inv_sum[part * 8 : (part + 1) * 8, :] += fold(hit)
        return carry

    lax.fori_loop(0, blocks, inverse_step, 0)
    for part in range(blocks):
        inverse[part : part + 1, :] = jnp.sum(
            inv_sum[part * 8 : (part + 1) * 8, :], axis=0, keepdims=True
        )
    for part in range(CHUNKS // 2):
        gather_forward(1, part)
    for part in range(CHUNKS // 2, CHUNKS):
        gather_forward(1, part)

    gather_finish(1)
    exchange(1)

    def second_apply(block, total):
        operand = direction[:, lane_tile(block)]
        mapped = apply_block(1, block, operand)
        res[:, lane_tile(block)] = mapped
        return total + operand * mapped

    dot_sum = lax.fori_loop(0, blocks, second_apply, nothing)
    reduce_begin(1, [norm_sum, dot_sum])
    reduce_middle(1)
    norm_last, dot_last, _ = reduce_end(1)
    second_step = norm_last / dot_last

    def output_step(tile, carry):
        columns = lane_tile(tile)
        right = sorted_loads[:, columns]
        sol[:, columns] = first_step * right + second_step * direction[:, columns]
        res[:, columns] = right - first_step * image[:, columns] - second_step * res[:, columns]
        return carry

    lax.fori_loop(0, blocks, output_step, 0)


def per_device(loads, coords, coreg_factor, noise, run_perm, block_nbrs, nbr_count):
    rows, runs = loads.shape
    blocks, slots = block_nbrs.shape
    samp_count = lax.axis_size("samp")
    halo = (slots - 1) * LANES
    extent = runs + 2 * halo
    chans = lax.axis_size("chan")
    vmem = pl.BlockSpec(memory_space=pltpu.VMEM)
    smem = pl.BlockSpec(memory_space=pltpu.SMEM)
    wide = pltpu.VMEM((rows, runs), F32)
    wide_out = jax.ShapeDtypeStruct((rows, runs), F32)
    index_rows = pltpu.VMEM((blocks, LANES), jnp.int32)
    limits = pltpu.CompilerParams(vmem_limit_bytes=48 * 2**20)
    perm = run_perm.reshape(blocks, LANES)
    sorted_loads, sorted_coords = pl.pallas_call(
        functools.partial(sorter, blocks),
        out_shape=[wide_out, jax.ShapeDtypeStruct((8, runs), F32)],
        in_specs=[vmem] * 3,
        out_specs=[vmem] * 2,
        scratch_shapes=[index_rows, pltpu.VMEM((8, runs), F32)],
        compiler_params=limits,
    )(loads, coords, perm)
    sorted_sol, sorted_res, inverse = pl.pallas_call(
        functools.partial(solver, samp_count, blocks, slots),
        out_shape=[wide_out, wide_out, jax.ShapeDtypeStruct((blocks, LANES), F32)],
        in_specs=[vmem] * 6 + [smem],
        out_specs=[vmem] * 3,
        scratch_shapes=[
            pltpu.VMEM((blocks * 8, LANES), F32),
            pltpu.VMEM((8, extent), F32),
            pltpu.VMEM((LANES, runs), BF16),
            pltpu.VMEM((extent // LANES, LANES, LANES), BF16),
            pltpu.VMEM((blocks, slots * LANES, LANES), BF16),
            pltpu.VMEM((chans, rows, coreg_factor.shape[1]), F32),
            pltpu.VMEM((3 * rows, chans * rows), BF16),
            wide, wide,
            pltpu.VMEM((2, chans, rows, runs), BF16),
            pltpu.VMEM((extent // LANES, rows, LANES), BF16),
            pltpu.VMEM((extent // LANES, rows, LANES), BF16),
            pltpu.VMEM((2, chans, 24, LANES), F32),
            pltpu.VMEM((2, samp_count, 24, LANES), F32),
            pltpu.SemaphoreType.DMA((3,)),
            pltpu.SemaphoreType.DMA((3,)),
            pltpu.SemaphoreType.DMA((2, 3, CHUNKS)),
            pltpu.SemaphoreType.DMA((2, 3, CHUNKS)),
            pltpu.SemaphoreType.DMA((3, 2)),
            pltpu.SemaphoreType.DMA((3, 2)),
            pltpu.SemaphoreType.DMA((2, 3)),
            pltpu.SemaphoreType.DMA((2, 3)),
            pltpu.SemaphoreType.DMA((2, samp_count)),
            pltpu.SemaphoreType.DMA((2, samp_count)),
        ],
        compiler_params=pltpu.CompilerParams(
            collective_id=0, has_side_effects=True, vmem_limit_bytes=56 * 2**20
        ),
    )(
        sorted_loads,
        sorted_coords,
        coreg_factor,
        noise[:, None],
        perm - lax.axis_index("samp") * runs,
        jnp.broadcast_to(nbr_count[:, None], (blocks, LANES)),
        block_nbrs[:, 0] - lax.axis_index("samp") * blocks + slots - 1,
    )
    return pl.pallas_call(
        functools.partial(unsorter, blocks),
        out_shape=[wide_out, wide_out],
        in_specs=[vmem] * 3,
        out_specs=[vmem] * 2,
        scratch_shapes=[index_rows],
        compiler_params=limits,
    )(sorted_sol, sorted_res, inverse)


def solution(mesh):
    return jax.shard_map(
        per_device,
        mesh=mesh,
        in_specs=(
            P("chan", "samp"),
            P(None, "samp"),
            P("chan", None),
            P("chan"),
            P("samp"),
            P("samp", None),
            P("samp"),
        ),
        out_specs=(P("chan", "samp"), P("chan", "samp")),
        check_vma=False,
    )
```

```python
import functools

import jax
import jax.numpy as jnp
from jax import lax
from jax.experimental import pallas as pl
from jax.experimental.pallas import tpu as pltpu
from jax.sharding import PartitionSpec as P

SUPPORT = 5.0
AMPLITUDE = 0.05
LANES = 128
CHUNKS = 4
MESH = pl.DeviceIdType.MESH
F32 = jnp.float32
BF16 = jnp.bfloat16


def lane_tile(index):
    return pl.ds(pl.multiple_of(index * LANES, LANES), LANES)


def pieces(value):
    high = value.astype(BF16).astype(F32)
    rest = value - high
    middle = rest.astype(BF16).astype(F32)
    return high, middle, (rest - middle).astype(BF16).astype(F32)


def fold(value):
    total = value[0:8]
    for row in range(8, value.shape[0], 8):
        total = total + value[row : row + 8]
    return total


def whole_sum(value):
    return jnp.sum(jnp.sum(value, axis=0, keepdims=True), axis=1, keepdims=True)


def solver(
    samp_count, blocks, slots,
    loads, coords, factor, noise, perm, nbrs, counts,
    sol, res,
    source, spread, sorted_loads, position, perm_rows, perm_column, image_out, coords_ext, own_terms, ext_terms, tiles,
    factors, coreg, direction, image, gathered, values_first, values_second,
    red_chan, red_samp,
    fac_send, fac_recv, gat_send, gat_recv, halo_send, halo_recv,
    rc_send, rc_recv, rs_send, rs_recv,
):
    rows, runs = loads.shape
    halo = (slots - 1) * LANES
    extent = runs + 2 * halo
    edge = slots - 1
    widened = blocks + 2 * edge
    values = (values_first, values_second)
    chunk = runs // CHUNKS
    samp = lax.axis_index("samp")
    chan = lax.axis_index("chan")
    core_peer = chan + 1 - 2 * (chan % 2)
    far_peer = (chan + 2) % 4
    chan_peers = (core_peer, far_peer, 3 - chan)

    barrier = pltpu.get_barrier_semaphore()
    for peer in chan_peers:
        pl.semaphore_signal(barrier, inc=1, device_id={"chan": peer}, device_id_type=MESH)

    def greet(hop, carry):
        pl.semaphore_signal(
            barrier, inc=1, device_id={"samp": (samp + hop) % samp_count}, device_id_type=MESH
        )
        return carry

    lax.fori_loop(1, samp_count, greet, 0)

    perm_rows[...] = perm[...] - samp * runs
    stride = 2 * LANES
    for begin in range(0, runs, stride):
        columns = slice(begin, begin + stride)
        parts = pieces(
            jnp.concatenate(
                [
                    loads[:, columns],
                    coords[:, columns] * (1.0 / SUPPORT),
                    jnp.zeros((8 - coords.shape[0], stride), F32),
                ],
                axis=0,
            )
        )
        source[:, columns] = jnp.concatenate(parts, axis=0).astype(BF16)
    depth = runs // 6
    for begin in range(0, depth, LANES):
        position[begin : begin + LANES, :] = (
            lax.broadcasted_iota(jnp.int32, (LANES, stride), 0) + begin
        )

    def sort_step(pair, carry):
        columns = pl.ds(pl.multiple_of(pair * stride, stride), stride)
        target = perm_rows[:, columns]
        total = jnp.zeros((3 * (rows + 8), stride), F32)
        for part in range(6):
            chosen = jnp.where(position[...] == target - part * depth, 1.0, 0.0).astype(BF16)
            total = total + jnp.dot(
                source[:, part * depth : (part + 1) * depth],
                chosen,
                preferred_element_type=F32,
            )
        high, middle, low = (total[n * (rows + 8) : (n + 1) * (rows + 8)] for n in range(3))
        result = high + middle + low
        sorted_loads[:, columns] = result[0:rows]
        coords_ext[:, pl.ds(pl.multiple_of(halo + pair * stride, LANES), stride)] = result[rows:]
        return carry

    def column_step(tile, carry):
        index = perm_rows[:, lane_tile(tile)].astype(F32)
        perm_column[lane_tile(tile), :] = jnp.broadcast_to(index, (LANES, LANES)).T
        return carry

    lane_id = lax.broadcasted_iota(jnp.int32, (1, LANES), 1).astype(F32)

    def unsort(block_sums, target):
        for begin in range(0, runs, stride):
            columns = slice(begin, begin + stride)
            high, middle, _ = pieces(block_sums[:, columns])
            spread[:, columns] = jnp.concatenate([high, middle], axis=0).astype(BF16)

        def unsort_step(pair, carry):
            columns = pl.ds(pl.multiple_of(pair * stride, stride), stride)
            low_lanes = lane_id + (pair * stride).astype(F32)
            total = jnp.zeros((2 * rows, stride), F32)
            for part in range(6):
                index = perm_column[part * depth : (part + 1) * depth, :]
                chosen = jnp.concatenate(
                    [
                        jnp.where(index == low_lanes, 1.0, 0.0).astype(BF16),
                        jnp.where(index == low_lanes + float(LANES), 1.0, 0.0).astype(BF16),
                    ],
                    axis=1,
                )
                total = total + jnp.dot(
                    spread[:, part * depth : (part + 1) * depth],
                    chosen,
                    preferred_element_type=F32,
                )
            target[:, columns] = total[0:rows] + total[rows:]
            return carry

        lax.fori_loop(0, runs // stride, unsort_step, 0)


    @pl.when(samp == 0)
    def _():
        coords_ext[:, 0:halo] = jnp.zeros((8, halo), F32)
        for turn in range(2):
            values[turn][0:edge] = jnp.zeros((edge, rows, LANES), BF16)

    @pl.when(samp == samp_count - 1)
    def _():
        coords_ext[:, extent - halo : extent] = jnp.zeros((8, halo), F32)
        for turn in range(2):
            values[turn][widened - edge : widened] = jnp.zeros((edge, rows, LANES), BF16)

    factors[chan] = factor[...]
    pl.semaphore_wait(barrier, 3 + samp_count - 1)

    def halo_copies(regions, turn):
        own_low, own_high, low, high = regions
        to_low = pltpu.make_async_remote_copy(
            src_ref=own_low,
            dst_ref=high,
            send_sem=halo_send.at[turn, 0],
            recv_sem=halo_recv.at[turn, 0],
            device_id={"samp": (samp + samp_count - 1) % samp_count},
            device_id_type=MESH,
        )
        to_high = pltpu.make_async_remote_copy(
            src_ref=own_high,
            dst_ref=low,
            send_sem=halo_send.at[turn, 1],
            recv_sem=halo_recv.at[turn, 1],
            device_id={"samp": (samp + 1) % samp_count},
            device_id_type=MESH,
        )
        return to_low, to_high

    def halo_start_low(copies):
        @pl.when(samp > 0)
        def _():
            copies[0].start()

    def halo_start_high(copies):
        @pl.when(samp < samp_count - 1)
        def _():
            copies[1].start()

    def halo_wait(copies):
        @pl.when(samp > 0)
        def _():
            copies[0].wait_send()
            copies[1].wait_recv()

        @pl.when(samp < samp_count - 1)
        def _():
            copies[1].wait_send()
            copies[0].wait_recv()

    factor_copies = []
    for relation, peer in enumerate(chan_peers):
        factor_copies.append(
            pltpu.make_async_remote_copy(
                src_ref=factors.at[chan],
                dst_ref=factors.at[chan],
                send_sem=fac_send.at[relation],
                recv_sem=fac_recv.at[relation],
                device_id={"chan": peer},
                device_id_type=MESH,
            )
        )
        factor_copies[-1].start()

    def gather_copy(turn, kind, part, owner, peer):
        place = gathered.at[turn, owner, :, pl.ds(part * chunk, chunk)]
        return pltpu.make_async_remote_copy(
            src_ref=place,
            dst_ref=place,
            send_sem=gat_send.at[turn, kind, part],
            recv_sem=gat_recv.at[turn, kind, part],
            device_id={"chan": peer},
            device_id_type=MESH,
        )

    def gather_start(turn, part):
        gather_copy(turn, 1, part, chan, far_peer).start()
        gather_copy(turn, 0, part, chan, core_peer).start()

    def gather_forward(turn, part):
        gather_copy(turn, 1, part, far_peer, far_peer).wait_recv()
        gather_copy(turn, 2, part, far_peer, core_peer).start()

    def gather_finish(turn):
        for part in range(CHUNKS):
            gather_copy(turn, 0, part, chan, core_peer).wait_send()
            gather_copy(turn, 1, part, chan, far_peer).wait_send()
            gather_copy(turn, 2, part, far_peer, core_peer).wait_send()
            gather_copy(turn, 0, part, core_peer, core_peer).wait_recv()
            gather_copy(turn, 2, part, 3 - chan, core_peer).wait_recv()

    per_chunk = blocks // CHUNKS
    pairs = runs // stride // CHUNKS
    for part in range(CHUNKS):
        lax.fori_loop(part * pairs, (part + 1) * pairs, sort_step, 0)
        columns = pl.ds(part * chunk, chunk)
        gathered[0, chan, :, columns] = sorted_loads[:, columns].astype(BF16)
        gather_start(0, part)

    coord_copies = halo_copies(
        [coords_ext.at[:, pl.ds(first, halo)] for first in (halo, runs, 0, extent - halo)], 0
    )
    halo_start_low(coord_copies)
    halo_start_high(coord_copies)

    row_id = lax.broadcasted_iota(jnp.int32, (8, LANES), 0)

    def own_step(tile, carry):
        point = coords_ext[:, lane_tile(tile + edge)]
        norm = jnp.sum(point * point, axis=0, keepdims=True)
        terms = jnp.where(row_id == 6, 1.0, jnp.where(row_id == 7, norm, -2.0 * point))
        high, middle, low = pieces(terms)
        stacked = jnp.concatenate(
            [high, middle, high, middle, low, high, jnp.zeros((LANES - 48, LANES), F32)], axis=0
        )
        own_terms[:, lane_tile(tile)] = stacked.astype(BF16)
        return carry

    lax.fori_loop(0, blocks, own_step, 0)
    halo_wait(coord_copies)

    def ext_step(tile, carry):
        point = coords_ext[:, lane_tile(tile)]
        norm = jnp.sum(point * point, axis=0, keepdims=True)
        terms = jnp.where(row_id == 6, norm, jnp.where(row_id == 7, 1.0, point))
        high, middle, low = pieces(terms)
        stacked = jnp.concatenate(
            [high, high, middle, middle, high, low, jnp.zeros((LANES - 48, LANES), F32)], axis=0
        )
        ext_terms[tile] = stacked.T.astype(BF16)
        return carry

    lax.fori_loop(0, extent // LANES, ext_step, 0)

    def window_start(block):
        return jnp.clip(nbrs[block, 0] - samp * blocks + edge, 0, widened - slots)

    def tile_step(block, carry):
        start = window_start(block)
        count = jnp.full((1, LANES), counts[block], jnp.int32)
        own = own_terms[:, lane_tile(block)]
        for slot in range(slots):
            partner = ext_terms[start + slot]
            squared = jnp.dot(partner, own, preferred_element_type=F32)
            squared = jnp.maximum(squared, 1e-20)
            radius = squared * lax.rsqrt(squared)
            live = jnp.where(count > slot, 1.0, 0.0)
            remain = jnp.maximum(live - radius, 0.0)
            cubed = remain * remain * remain
            tile = cubed * cubed * (6.0 * radius + 1.0)
            tiles[block, slot * LANES : (slot + 1) * LANES, :] = tile.astype(BF16)
        return carry

    first_part = (blocks * 5) // 8
    lax.fori_loop(0, first_part, tile_step, 0)
    for part in range(CHUNKS):
        gather_forward(0, part)
    lax.fori_loop(first_part, blocks, tile_step, 0)

    for copy in factor_copies:
        copy.wait()
    coreg_rows = lax.dot_general(
        factor[...],
        factors[...].reshape(4 * rows, factor.shape[1]),
        (((1,), (1,)), ((), ())),
        precision=lax.Precision.HIGHEST,
        preferred_element_type=F32,
    )
    for number, piece in enumerate(pieces(coreg_rows)):
        coreg[number * rows : (number + 1) * rows, :] = piece.astype(BF16)

    def mix(turn, begin, end):
        weights = coreg[...]
        while begin < end:
            width = min(2 * LANES, end - begin)
            operand = gathered[turn, :, :, begin : begin + width].reshape(4 * rows, width)
            product = jnp.dot(weights, operand, preferred_element_type=F32)
            mixed = product[0:rows] + product[rows : 2 * rows] + product[2 * rows : 3 * rows]
            for part in range(width // LANES):
                values[turn][edge + begin // LANES + part] = mixed[
                    :, part * LANES : (part + 1) * LANES
                ].astype(BF16)
            begin += width

    def exchange(turn):
        copies = halo_copies(
            [
                values[turn].at[pl.ds(first, edge)]
                for first in (edge, blocks, 0, widened - edge)
            ],
            turn + 1,
        )
        mix(turn, 0, halo)
        halo_start_low(copies)
        if runs - halo >= halo:
            mix(turn, runs - halo, runs)
            halo_start_high(copies)
            mix(turn, halo, runs - halo)
        halo_wait(copies)

    diagonal = lax.broadcasted_iota(jnp.int32, (rows, rows), 0) == lax.broadcasted_iota(
        jnp.int32, (rows, rows), 1
    )
    noise_column = jnp.sum(jnp.where(diagonal, noise[...], 0.0), axis=1, keepdims=True)
    noise_wide = jnp.broadcast_to(noise_column, (rows, LANES))
    nothing = jnp.zeros((rows, LANES), F32)

    def apply_block(turn, block, operand):
        start = window_start(block)
        partner = jnp.concatenate([values[turn][start + slot] for slot in range(slots)], axis=1)
        summed = jnp.dot(partner, tiles[block], preferred_element_type=F32)
        return AMPLITUDE * summed + noise_wide * operand

    def reduce_chan_copy(turn, relation, owner, peer):
        return pltpu.make_async_remote_copy(
            src_ref=red_chan.at[turn, owner],
            dst_ref=red_chan.at[turn, owner],
            send_sem=rc_send.at[turn, relation],
            recv_sem=rc_recv.at[turn, relation],
            device_id={"chan": peer},
            device_id_type=MESH,
        )

    def reduce_begin(turn, parts):
        for number, part in enumerate(parts):
            red_chan[turn, chan, number * 8 : (number + 1) * 8, :] = fold(part)
        for number in range(len(parts), 3):
            red_chan[turn, chan, number * 8 : (number + 1) * 8, :] = jnp.zeros((8, LANES), F32)
        for relation, peer in enumerate(chan_peers):
            reduce_chan_copy(turn, relation, chan, peer).start()

    def reduce_samp_copy(turn, hop, owner):
        return pltpu.make_async_remote_copy(
            src_ref=red_samp.at[turn, owner],
            dst_ref=red_samp.at[turn, owner],
            send_sem=rs_send.at[turn, hop],
            recv_sem=rs_recv.at[turn, owner],
            device_id={"samp": (samp + hop) % samp_count},
            device_id_type=MESH,
        )

    def reduce_middle(turn):
        for relation, peer in enumerate(chan_peers):
            reduce_chan_copy(turn, relation, chan, peer).wait_send()
            reduce_chan_copy(turn, relation, peer, peer).wait_recv()
        total = red_chan[turn, 0] + red_chan[turn, 1] + red_chan[turn, 2] + red_chan[turn, 3]
        red_samp[turn, samp] = total

        def send(hop, carry):
            reduce_samp_copy(turn, hop, samp).start()
            return carry

        lax.fori_loop(1, samp_count, send, 0)

    def reduce_end(turn):
        def wait(hop, carry):
            reduce_samp_copy(turn, hop, samp).wait_send()
            reduce_samp_copy(turn, hop, (samp + hop) % samp_count).wait_recv()
            return carry

        lax.fori_loop(1, samp_count, wait, 0)

        def add(index, total):
            return total + red_samp[turn, index]

        total = lax.fori_loop(0, samp_count, add, jnp.zeros((24, LANES), F32))
        return [whole_sum(total[number * 8 : (number + 1) * 8]) for number in range(3)]

    gather_finish(0)
    exchange(0)

    def first_apply(block, carry):
        norm, dot, square = carry
        operand = sorted_loads[:, lane_tile(block)]
        mapped = apply_block(0, block, operand)
        image[:, lane_tile(block)] = mapped
        return norm + operand * operand, dot + operand * mapped, square + mapped * mapped

    sums = lax.fori_loop(0, blocks, first_apply, (nothing, nothing, nothing))
    reduce_begin(0, sums)
    reduce_middle(0)
    norm_now, dot, square = reduce_end(0)
    first_step = norm_now / dot
    norm_next = jnp.maximum(
        norm_now - 2.0 * first_step * dot + first_step * first_step * square, 0.0
    )
    ratio = norm_next / norm_now

    norm_sum = nothing
    for part in range(CHUNKS):
        for tile in range(part * per_chunk, (part + 1) * per_chunk):
            columns = slice(tile * LANES, (tile + 1) * LANES)
            operand = sorted_loads[:, columns]
            remainder = operand - first_step * image[:, columns]
            norm_sum = norm_sum + remainder * remainder
            step = remainder + ratio * operand
            direction[:, columns] = step
            gathered[1, chan, :, columns] = step.astype(BF16)
        gather_start(1, part)

    lax.fori_loop(0, blocks, column_step, 0)
    for part in range(CHUNKS // 2):
        gather_forward(1, part)
    unsort(image, image_out)
    for part in range(CHUNKS // 2, CHUNKS):
        gather_forward(1, part)

    gather_finish(1)
    exchange(1)

    def second_apply(block, total):
        operand = direction[:, lane_tile(block)]
        mapped = apply_block(1, block, operand)
        image[:, lane_tile(block)] = mapped
        return total + operand * mapped

    dot_sum = lax.fori_loop(0, blocks, second_apply, nothing)
    reduce_begin(1, [norm_sum, dot_sum])
    reduce_middle(1)
    unsort(image, direction)
    norm_last, dot_last, _ = reduce_end(1)
    second_step = norm_last / dot_last

    def output_step(tile, carry):
        columns = lane_tile(tile)
        right = loads[:, columns]
        remainder = right - first_step * image_out[:, columns]
        step = remainder + ratio * right
        sol[:, columns] = first_step * right + second_step * step
        res[:, columns] = remainder - second_step * direction[:, columns]
        return carry

    lax.fori_loop(0, blocks, output_step, 0)


def per_device(loads, coords, coreg_factor, noise, run_perm, block_nbrs, nbr_count):
    rows, runs = loads.shape
    blocks, slots = block_nbrs.shape
    samp_count = lax.axis_size("samp")
    halo = (slots - 1) * LANES
    extent = runs + 2 * halo
    chans = lax.axis_size("chan")
    vmem = pl.BlockSpec(memory_space=pltpu.VMEM)
    smem = pl.BlockSpec(memory_space=pltpu.SMEM)
    wide = pltpu.VMEM((rows, runs), F32)
    wide_out = jax.ShapeDtypeStruct((rows, runs), F32)
    return pl.pallas_call(
        functools.partial(solver, samp_count, blocks, slots),
        out_shape=[wide_out, wide_out],
        in_specs=[vmem] * 5 + [smem] * 2,
        out_specs=[vmem] * 2,
        scratch_shapes=[
            pltpu.VMEM((3 * (rows + 8), runs), BF16),
            pltpu.VMEM((2 * rows, runs), BF16),
            wide,
            pltpu.VMEM((runs // 6, 2 * LANES), jnp.int32),
            pltpu.VMEM((1, runs), jnp.int32),
            pltpu.VMEM((runs, LANES), F32),
            wide,
            pltpu.VMEM((8, extent), F32),
            pltpu.VMEM((LANES, runs), BF16),
            pltpu.VMEM((extent // LANES, LANES, LANES), BF16),
            pltpu.VMEM((blocks, slots * LANES, LANES), BF16),
            pltpu.VMEM((chans, rows, coreg_factor.shape[1]), F32),
            pltpu.VMEM((3 * rows, chans * rows), BF16),
            wide, wide,
            pltpu.VMEM((2, chans, rows, runs), BF16),
            pltpu.VMEM((extent // LANES, rows, LANES), BF16),
            pltpu.VMEM((extent // LANES, rows, LANES), BF16),
            pltpu.VMEM((2, chans, 24, LANES), F32),
            pltpu.VMEM((2, samp_count, 24, LANES), F32),
            pltpu.SemaphoreType.DMA((3,)),
            pltpu.SemaphoreType.DMA((3,)),
            pltpu.SemaphoreType.DMA((2, 3, CHUNKS)),
            pltpu.SemaphoreType.DMA((2, 3, CHUNKS)),
            pltpu.SemaphoreType.DMA((3, 2)),
            pltpu.SemaphoreType.DMA((3, 2)),
            pltpu.SemaphoreType.DMA((2, 3)),
            pltpu.SemaphoreType.DMA((2, 3)),
            pltpu.SemaphoreType.DMA((2, samp_count)),
            pltpu.SemaphoreType.DMA((2, samp_count)),
        ],
        compiler_params=pltpu.CompilerParams(
            collective_id=0, has_side_effects=True, vmem_limit_bytes=56 * 2**20
        ),
    )(
        loads,
        coords,
        coreg_factor,
        noise[None, :],
        run_perm[None, :],
        block_nbrs,
        nbr_count,
    )


def solution(mesh):
    return jax.shard_map(
        per_device,
        mesh=mesh,
        in_specs=(
            P("chan", "samp"),
            P(None, "samp"),
            P("chan", None),
            P("chan"),
            P("samp"),
            P("samp", None),
            P("samp"),
        ),
        out_specs=(P("chan", "samp"), P("chan", "samp")),
        check_vma=False,
    )
```

```python
import functools

import jax
import jax.numpy as jnp
from jax import lax
from jax.experimental import pallas as pl
from jax.experimental.pallas import tpu as pltpu
from jax.sharding import PartitionSpec as P

SUPPORT = 5.0
AMPLITUDE = 0.05
LANES = 128
CHUNKS = 4
MESH = pl.DeviceIdType.MESH
F32 = jnp.float32
BF16 = jnp.bfloat16


def lane_tile(index):
    return pl.ds(pl.multiple_of(index * LANES, LANES), LANES)


def pieces(value):
    high = value.astype(BF16).astype(F32)
    rest = value - high
    middle = rest.astype(BF16).astype(F32)
    return high, middle, (rest - middle).astype(BF16).astype(F32)


def fold(value):
    total = value[0:8]
    for row in range(8, value.shape[0], 8):
        total = total + value[row : row + 8]
    return total


def whole_sum(value):
    return jnp.sum(jnp.sum(value, axis=0, keepdims=True), axis=1, keepdims=True)


def solver(
    samp_count, blocks, slots,
    loads, coords, factor, noise, perm, nbrs, counts,
    image_out, second_out, scalars,
    source, spread, sorted_loads, position, perm_rows, perm_column, coords_ext, own_terms, ext_terms, tiles,
    factors, coreg, direction, image, gathered, values_first, values_second,
    red_chan, red_samp,
    fac_send, fac_recv, gat_send, gat_recv, halo_send, halo_recv,
    rc_send, rc_recv, rs_send, rs_recv,
):
    rows, runs = loads.shape
    halo = (slots - 1) * LANES
    extent = runs + 2 * halo
    edge = slots - 1
    widened = blocks + 2 * edge
    values = (values_first, values_second)
    chunk = runs // CHUNKS
    samp = lax.axis_index("samp")
    chan = lax.axis_index("chan")
    core_peer = chan + 1 - 2 * (chan % 2)
    far_peer = (chan + 2) % 4
    chan_peers = (core_peer, far_peer, 3 - chan)

    barrier = pltpu.get_barrier_semaphore()
    for peer in chan_peers:
        pl.semaphore_signal(barrier, inc=1, device_id={"chan": peer}, device_id_type=MESH)

    def greet(hop, carry):
        pl.semaphore_signal(
            barrier, inc=1, device_id={"samp": (samp + hop) % samp_count}, device_id_type=MESH
        )
        return carry

    lax.fori_loop(1, samp_count, greet, 0)

    perm_rows[...] = perm[...] - samp * runs
    stride = 2 * LANES
    for begin in range(0, runs, stride):
        columns = slice(begin, begin + stride)
        parts = pieces(
            jnp.concatenate(
                [
                    loads[:, columns],
                    coords[:, columns] * (1.0 / SUPPORT),
                    jnp.zeros((8 - coords.shape[0], stride), F32),
                ],
                axis=0,
            )
        )
        source[:, columns] = jnp.concatenate(parts, axis=0).astype(BF16)
    depth = runs // 6
    for begin in range(0, depth, LANES):
        position[begin : begin + LANES, :] = (
            lax.broadcasted_iota(jnp.int32, (LANES, stride), 0) + begin
        )

    def sort_step(pair, carry):
        columns = pl.ds(pl.multiple_of(pair * stride, stride), stride)
        target = perm_rows[:, columns]
        total = jnp.zeros((3 * (rows + 8), stride), F32)
        for part in range(6):
            chosen = jnp.where(position[...] == target - part * depth, 1.0, 0.0).astype(BF16)
            total = total + jnp.dot(
                source[:, part * depth : (part + 1) * depth],
                chosen,
                preferred_element_type=F32,
            )
        high, middle, low = (total[n * (rows + 8) : (n + 1) * (rows + 8)] for n in range(3))
        result = high + middle + low
        sorted_loads[:, columns] = result[0:rows]
        coords_ext[:, pl.ds(pl.multiple_of(halo + pair * stride, LANES), stride)] = result[rows:]
        return carry

    def column_step(tile, carry):
        index = perm_rows[:, lane_tile(tile)].astype(F32)
        perm_column[lane_tile(tile), :] = jnp.broadcast_to(index, (LANES, LANES)).T
        return carry

    lane_id = lax.broadcasted_iota(jnp.int32, (1, LANES), 1).astype(F32)

    def unsort_begin(block_sums):
        for begin in range(0, runs, stride):
            columns = slice(begin, begin + stride)
            high, middle, _ = pieces(block_sums[:, columns])
            spread[:, columns] = jnp.concatenate([high, middle], axis=0).astype(BF16)

    def unsort(target, begin, end):
        def unsort_step(pair, carry):
            columns = pl.ds(pl.multiple_of(pair * stride, stride), stride)
            low_lanes = lane_id + (pair * stride).astype(F32)
            total = jnp.zeros((2 * rows, stride), F32)
            for part in range(6):
                index = perm_column[part * depth : (part + 1) * depth, :]
                chosen = jnp.concatenate(
                    [
                        jnp.where(index == low_lanes, 1.0, 0.0).astype(BF16),
                        jnp.where(index == low_lanes + float(LANES), 1.0, 0.0).astype(BF16),
                    ],
                    axis=1,
                )
                total = total + jnp.dot(
                    spread[:, part * depth : (part + 1) * depth],
                    chosen,
                    preferred_element_type=F32,
                )
            target[:, columns] = total[0:rows] + total[rows:]
            return carry

        lax.fori_loop(begin, end, unsort_step, 0)


    @pl.when(samp == 0)
    def _():
        coords_ext[:, 0:halo] = jnp.zeros((8, halo), F32)
        for turn in range(2):
            values[turn][0:edge] = jnp.zeros((edge, rows, LANES), BF16)

    @pl.when(samp == samp_count - 1)
    def _():
        coords_ext[:, extent - halo : extent] = jnp.zeros((8, halo), F32)
        for turn in range(2):
            values[turn][widened - edge : widened] = jnp.zeros((edge, rows, LANES), BF16)

    factors[chan] = factor[...]
    pl.semaphore_wait(barrier, 3 + samp_count - 1)

    per_chunk = blocks // CHUNKS
    below = (samp + samp_count - 1) % samp_count
    above = (samp + 1) % samp_count

    def halo_copy(source_ref, target_ref, turn, side, part):
        return pltpu.make_async_remote_copy(
            src_ref=source_ref,
            dst_ref=target_ref,
            send_sem=halo_send.at[turn, side, part],
            recv_sem=halo_recv.at[turn, side, part],
            device_id={"samp": below if side == 0 else above},
            device_id_type=MESH,
        )

    def halo_start(copies):
        for side, group in enumerate(copies):
            if group:
                @pl.when((samp > 0) if side == 0 else (samp < samp_count - 1))
                def _():
                    for copy in group:
                        copy.start()

    def halo_wait(copies):
        @pl.when(samp > 0)
        def _():
            for copy in copies[0]:
                copy.wait_send()
            for copy in copies[1]:
                copy.wait_recv()

        @pl.when(samp < samp_count - 1)
        def _():
            for copy in copies[1]:
                copy.wait_send()
            for copy in copies[0]:
                copy.wait_recv()

    def value_copies(turn, part):
        buffer = values[turn]
        begin, end = part * per_chunk, (part + 1) * per_chunk
        result = ([], [])
        if begin < edge:
            count = min(end, edge) - begin
            result[0].append(
                halo_copy(
                    buffer.at[pl.ds(edge + begin, count)],
                    buffer.at[pl.ds(edge + blocks + begin, count)],
                    turn + 1, 0, part,
                )
            )
        if end > blocks - edge:
            first = max(begin, blocks - edge)
            result[1].append(
                halo_copy(
                    buffer.at[pl.ds(edge + first, end - first)],
                    buffer.at[pl.ds(edge + first - blocks, end - first)],
                    turn + 1, 1, part,
                )
            )
        return result

    factor_copies = []
    for relation, peer in enumerate(chan_peers):
        factor_copies.append(
            pltpu.make_async_remote_copy(
                src_ref=factors.at[chan],
                dst_ref=factors.at[chan],
                send_sem=fac_send.at[relation],
                recv_sem=fac_recv.at[relation],
                device_id={"chan": peer},
                device_id_type=MESH,
            )
        )
        factor_copies[-1].start()

    def gather_copy(turn, kind, part, owner, peer):
        place = gathered.at[turn, owner, :, pl.ds(part * chunk, chunk)]
        return pltpu.make_async_remote_copy(
            src_ref=place,
            dst_ref=place,
            send_sem=gat_send.at[turn, kind, part],
            recv_sem=gat_recv.at[turn, kind, part],
            device_id={"chan": peer},
            device_id_type=MESH,
        )

    def gather_start(turn, part):
        gather_copy(turn, 1, part, chan, far_peer).start()
        gather_copy(turn, 0, part, chan, core_peer).start()

    def gather_forward(turn, part):
        gather_copy(turn, 1, part, far_peer, far_peer).wait_recv()
        gather_copy(turn, 2, part, far_peer, core_peer).start()

    def gather_finish(turn, part):
        gather_copy(turn, 0, part, chan, core_peer).wait_send()
        gather_copy(turn, 1, part, chan, far_peer).wait_send()
        gather_copy(turn, 2, part, far_peer, core_peer).wait_send()
        gather_copy(turn, 0, part, core_peer, core_peer).wait_recv()
        gather_copy(turn, 2, part, 3 - chan, core_peer).wait_recv()

    pairs = runs // stride // CHUNKS
    for part in range(CHUNKS):
        lax.fori_loop(part * pairs, (part + 1) * pairs, sort_step, 0)
        columns = pl.ds(part * chunk, chunk)
        gathered[0, chan, :, columns] = sorted_loads[:, columns].astype(BF16)
        gather_start(0, part)

    coord_copies = (
        [halo_copy(
            coords_ext.at[:, pl.ds(halo, halo)],
            coords_ext.at[:, pl.ds(extent - halo, halo)],
            0, 0, 0,
        )],
        [halo_copy(
            coords_ext.at[:, pl.ds(runs, halo)], coords_ext.at[:, pl.ds(0, halo)], 0, 1, 0
        )],
    )
    halo_start(coord_copies)

    row_id = lax.broadcasted_iota(jnp.int32, (8, LANES), 0)

    def own_step(tile, carry):
        point = coords_ext[:, lane_tile(tile + edge)]
        norm = jnp.sum(point * point, axis=0, keepdims=True)
        terms = jnp.where(row_id == 6, 1.0, jnp.where(row_id == 7, norm, -2.0 * point))
        high, middle, low = pieces(terms)
        stacked = jnp.concatenate(
            [high, middle, high, middle, low, high, jnp.zeros((LANES - 48, LANES), F32)], axis=0
        )
        own_terms[:, lane_tile(tile)] = stacked.astype(BF16)
        return carry

    lax.fori_loop(0, blocks, own_step, 0)
    halo_wait(coord_copies)

    def ext_step(tile, carry):
        point = coords_ext[:, lane_tile(tile)]
        norm = jnp.sum(point * point, axis=0, keepdims=True)
        terms = jnp.where(row_id == 6, norm, jnp.where(row_id == 7, 1.0, point))
        high, middle, low = pieces(terms)
        stacked = jnp.concatenate(
            [high, high, middle, middle, high, low, jnp.zeros((LANES - 48, LANES), F32)], axis=0
        )
        ext_terms[tile] = stacked.T.astype(BF16)
        return carry

    lax.fori_loop(0, extent // LANES, ext_step, 0)

    def window_start(block):
        return jnp.clip(nbrs[0, block] - samp * blocks + edge, 0, widened - slots)

    def tile_step(block, carry):
        start = window_start(block)
        count = jnp.full((1, LANES), counts[block], jnp.int32)
        own = own_terms[:, lane_tile(block)]
        for slot in range(slots):
            partner = ext_terms[start + slot]
            squared = jnp.dot(partner, own, preferred_element_type=F32)
            squared = jnp.maximum(squared, 1e-20)
            radius = squared * lax.rsqrt(squared)
            live = jnp.where(count > slot, 1.0, 0.0)
            remain = jnp.maximum(live - radius, 0.0)
            cubed = remain * remain * remain
            tile = cubed * cubed * (6.0 * radius + 1.0)
            tiles[block, slot * LANES : (slot + 1) * LANES, :] = tile.astype(BF16)
        return carry

    for copy in factor_copies:
        copy.wait()
    coreg_rows = lax.dot_general(
        factor[...],
        factors[...].reshape(4 * rows, factor.shape[1]),
        (((1,), (1,)), ((), ())),
        precision=lax.Precision.HIGHEST,
        preferred_element_type=F32,
    )
    for number, piece in enumerate(pieces(coreg_rows)):
        coreg[number * rows : (number + 1) * rows, :] = piece.astype(BF16)

    def mix(turn, part):
        gather_finish(turn, part)
        for begin in range(part * chunk, (part + 1) * chunk, stride):
            operand = gathered[turn, :, :, begin : begin + stride].reshape(4 * rows, stride)
            product = jnp.dot(coreg[...], operand, preferred_element_type=F32)
            mixed = product[0:rows] + product[rows : 2 * rows] + product[2 * rows : 3 * rows]
            for half in range(2):
                values[turn][edge + begin // LANES + half] = mixed[
                    :, half * LANES : (half + 1) * LANES
                ].astype(BF16)
        copies = value_copies(turn, part)
        halo_start(copies)
        return copies

    def merge(groups):
        return tuple([copy for group in groups for copy in group[side]] for side in range(2))

    diagonal = lax.broadcasted_iota(jnp.int32, (rows, rows), 0) == lax.broadcasted_iota(
        jnp.int32, (rows, rows), 1
    )
    noise_column = jnp.sum(jnp.where(diagonal, noise[...], 0.0), axis=1, keepdims=True)
    noise_wide = jnp.broadcast_to(noise_column, (rows, LANES))
    nothing = jnp.zeros((rows, LANES), F32)

    def apply_block(turn, block, operand):
        start = window_start(block)
        partner = jnp.concatenate([values[turn][start + slot] for slot in range(slots)], axis=1)
        summed = jnp.dot(partner, tiles[block], preferred_element_type=F32)
        return AMPLITUDE * summed + noise_wide * operand

    def reduce_chan_copy(turn, relation, owner, peer):
        return pltpu.make_async_remote_copy(
            src_ref=red_chan.at[turn, owner],
            dst_ref=red_chan.at[turn, owner],
            send_sem=rc_send.at[turn, relation],
            recv_sem=rc_recv.at[turn, relation],
            device_id={"chan": peer},
            device_id_type=MESH,
        )

    def reduce_begin(turn, parts):
        lines = []
        for part in parts:
            lines.append(jnp.sum(fold(part), axis=0, keepdims=True))
        lines.append(jnp.zeros((8 - len(parts), LANES), F32))
        red_chan[turn, chan] = jnp.concatenate(lines, axis=0)
        for relation, peer in enumerate(chan_peers):
            reduce_chan_copy(turn, relation, chan, peer).start()

    def reduce_samp_copy(turn, hop, owner):
        return pltpu.make_async_remote_copy(
            src_ref=red_samp.at[turn, owner],
            dst_ref=red_samp.at[turn, owner],
            send_sem=rs_send.at[turn, hop],
            recv_sem=rs_recv.at[turn, owner],
            device_id={"samp": (samp + hop) % samp_count},
            device_id_type=MESH,
        )

    def reduce_middle(turn):
        for relation, peer in enumerate(chan_peers):
            reduce_chan_copy(turn, relation, chan, peer).wait_send()
            reduce_chan_copy(turn, relation, peer, peer).wait_recv()
        total = red_chan[turn, 0] + red_chan[turn, 1] + red_chan[turn, 2] + red_chan[turn, 3]
        red_samp[turn, samp] = total

        def send(hop, carry):
            reduce_samp_copy(turn, hop, samp).start()
            return carry

        lax.fori_loop(1, samp_count, send, 0)

    def reduce_end(turn):
        def wait(hop, carry):
            reduce_samp_copy(turn, hop, samp).wait_send()
            reduce_samp_copy(turn, hop, (samp + hop) % samp_count).wait_recv()
            return carry

        lax.fori_loop(1, samp_count, wait, 0)

        def add(index, total):
            return total + red_samp[turn, index]

        total = lax.fori_loop(0, samp_count, add, jnp.zeros((8, LANES), F32))
        return [whole_sum(total[number : number + 1]) for number in range(3)]

    eighth = blocks // 8
    lax.fori_loop(0, eighth, tile_step, 0)
    gather_forward(0, 0)
    gather_forward(0, 1)
    lax.fori_loop(eighth, 2 * eighth, tile_step, 0)
    gather_forward(0, 2)
    gather_forward(0, 3)
    lax.fori_loop(2 * eighth, 3 * eighth, tile_step, 0)
    copies = [mix(0, 0), mix(0, 1), mix(0, 2), mix(0, 3)]
    lax.fori_loop(3 * eighth, blocks, tile_step, 0)
    halo_wait(merge(copies))

    def first_apply(block, carry):
        norm, dot, square = carry
        operand = sorted_loads[:, lane_tile(block)]
        mapped = apply_block(0, block, operand)
        image[:, lane_tile(block)] = mapped
        return norm + operand * operand, dot + operand * mapped, square + mapped * mapped

    sums = lax.fori_loop(0, blocks, first_apply, (nothing, nothing, nothing))
    reduce_begin(0, sums)
    reduce_middle(0)
    norm_now, dot, square = reduce_end(0)
    first_step = norm_now / dot
    norm_next = jnp.maximum(
        norm_now - 2.0 * first_step * dot + first_step * first_step * square, 0.0
    )
    ratio = norm_next / norm_now

    norm_sum = nothing
    for part in range(CHUNKS):
        for tile in range(part * per_chunk, (part + 1) * per_chunk):
            columns = slice(tile * LANES, (tile + 1) * LANES)
            operand = sorted_loads[:, columns]
            remainder = operand - first_step * image[:, columns]
            norm_sum = norm_sum + remainder * remainder
            step = remainder + ratio * operand
            direction[:, columns] = step
            gathered[1, chan, :, columns] = step.astype(BF16)
        gather_start(1, part)

    lax.fori_loop(0, blocks, column_step, 0)
    unsort_begin(image)
    copies = []
    for part in range(CHUNKS):
        unsort(image_out, part * pairs, (part + 1) * pairs)
        gather_forward(1, part)
        if part:
            copies.append(mix(1, part - 1))
    copies.append(mix(1, CHUNKS - 1))
    halo_wait(merge(copies))

    def second_apply(block, total):
        operand = direction[:, lane_tile(block)]
        mapped = apply_block(1, block, operand)
        image[:, lane_tile(block)] = mapped
        return total + operand * mapped

    dot_sum = lax.fori_loop(0, blocks, second_apply, nothing)
    reduce_begin(1, [norm_sum, dot_sum])
    reduce_middle(1)
    unsort_begin(image)
    unsort(second_out, 0, runs // stride)
    norm_last, dot_last, _ = reduce_end(1)
    second_step = norm_last / dot_last
    scalars[0:1, :] = jnp.broadcast_to(first_step, (1, LANES))
    scalars[1:2, :] = jnp.broadcast_to(ratio, (1, LANES))
    scalars[2:8, :] = jnp.broadcast_to(second_step, (6, LANES))


def per_device(loads, coords, coreg_factor, noise, run_perm, block_nbrs, nbr_count):
    rows, runs = loads.shape
    blocks, slots = block_nbrs.shape
    samp_count = lax.axis_size("samp")
    halo = (slots - 1) * LANES
    extent = runs + 2 * halo
    chans = lax.axis_size("chan")
    vmem = pl.BlockSpec(memory_space=pltpu.VMEM)
    smem = pl.BlockSpec(memory_space=pltpu.SMEM)
    wide = pltpu.VMEM((rows, runs), F32)
    wide_out = jax.ShapeDtypeStruct((rows, runs), F32)
    image, second_image, scalars = pl.pallas_call(
        functools.partial(solver, samp_count, blocks, slots),
        out_shape=[wide_out, wide_out, jax.ShapeDtypeStruct((8, LANES), F32)],
        in_specs=[vmem] * 5 + [smem] * 2,
        out_specs=[vmem] * 3,
        scratch_shapes=[
            pltpu.VMEM((3 * (rows + 8), runs), BF16),
            pltpu.VMEM((2 * rows, runs), BF16),
            wide,
            pltpu.VMEM((runs // 6, 2 * LANES), jnp.int32),
            pltpu.VMEM((1, runs), jnp.int32),
            pltpu.VMEM((runs, LANES), F32),
            pltpu.VMEM((8, extent), F32),
            pltpu.VMEM((LANES, runs), BF16),
            pltpu.VMEM((extent // LANES, LANES, LANES), BF16),
            pltpu.VMEM((blocks, slots * LANES, LANES), BF16),
            pltpu.VMEM((chans, rows, coreg_factor.shape[1]), F32),
            pltpu.VMEM((3 * rows, chans * rows), BF16),
            wide, wide,
            pltpu.VMEM((2, chans, rows, runs), BF16),
            pltpu.VMEM((extent // LANES, rows, LANES), BF16),
            pltpu.VMEM((extent // LANES, rows, LANES), BF16),
            pltpu.VMEM((2, chans, 8, LANES), F32),
            pltpu.VMEM((2, samp_count, 8, LANES), F32),
            pltpu.SemaphoreType.DMA((3,)),
            pltpu.SemaphoreType.DMA((3,)),
            pltpu.SemaphoreType.DMA((2, 3, CHUNKS)),
            pltpu.SemaphoreType.DMA((2, 3, CHUNKS)),
            pltpu.SemaphoreType.DMA((3, 2, CHUNKS)),
            pltpu.SemaphoreType.DMA((3, 2, CHUNKS)),
            pltpu.SemaphoreType.DMA((2, 3)),
            pltpu.SemaphoreType.DMA((2, 3)),
            pltpu.SemaphoreType.DMA((2, samp_count)),
            pltpu.SemaphoreType.DMA((2, samp_count)),
        ],
        compiler_params=pltpu.CompilerParams(
            collective_id=0, has_side_effects=True, vmem_limit_bytes=56 * 2**20
        ),
    )(
        loads,
        coords,
        coreg_factor,
        noise[None, :],
        run_perm[None, :],
        block_nbrs.T,
        nbr_count,
    )
    first_step, ratio, second_step = scalars[0, 0], scalars[1, 0], scalars[2, 0]
    remainder = loads - first_step * image
    step = remainder + ratio * loads
    return first_step * loads + second_step * step, remainder - second_step * second_image


def solution(mesh):
    return jax.shard_map(
        per_device,
        mesh=mesh,
        in_specs=(
            P("chan", "samp"),
            P(None, "samp"),
            P("chan", None),
            P("chan"),
            P("samp"),
            P("samp", None),
            P("samp"),
        ),
        out_specs=(P("chan", "samp"), P("chan", "samp")),
        check_vma=False,
    )
```

```python
import functools

import jax
import jax.numpy as jnp
from jax import lax
from jax.experimental import pallas as pl
from jax.experimental.pallas import tpu as pltpu
from jax.sharding import PartitionSpec as P

SUPPORT = 5.0
AMPLITUDE = 0.05
LANES = 128
CHUNKS = 4
MESH = pl.DeviceIdType.MESH
F32 = jnp.float32
BF16 = jnp.bfloat16


def lane_tile(index):
    return pl.ds(pl.multiple_of(index * LANES, LANES), LANES)


def pieces(value):
    high = value.astype(BF16).astype(F32)
    rest = value - high
    middle = rest.astype(BF16).astype(F32)
    return high, middle, (rest - middle).astype(BF16).astype(F32)


def fold(value):
    total = value[0:8]
    for row in range(8, value.shape[0], 8):
        total = total + value[row : row + 8]
    return total


def whole_sum(value):
    return jnp.sum(jnp.sum(value, axis=0, keepdims=True), axis=1, keepdims=True)


def solver(
    samp_count, blocks, slots,
    loads, coords, factor, noise, perm, nbrs, counts,
    image_out, second_out, scalars,
    source, spread, sorted_loads, position, perm_rows, perm_column, coords_ext, own_terms, ext_terms, tiles,
    factors, coreg, direction, image, gathered, values_first, values_second,
    red_chan, red_samp,
    fac_send, fac_recv, gat_send, gat_recv, halo_send, halo_recv,
    rc_send, rc_recv, rs_send, rs_recv,
):
    rows, runs = loads.shape
    halo = (slots - 1) * LANES
    extent = runs + 2 * halo
    edge = slots - 1
    widened = blocks + 2 * edge
    values = (values_first, values_second)
    chunk = runs // CHUNKS
    samp = lax.axis_index("samp")
    chan = lax.axis_index("chan")
    core_peer = chan + 1 - 2 * (chan % 2)
    far_peer = (chan + 2) % 4
    chan_peers = (core_peer, far_peer, 3 - chan)

    barrier = pltpu.get_barrier_semaphore()
    for peer in chan_peers:
        pl.semaphore_signal(barrier, inc=1, device_id={"chan": peer}, device_id_type=MESH)

    def greet(hop, carry):
        pl.semaphore_signal(
            barrier, inc=1, device_id={"samp": (samp + hop) % samp_count}, device_id_type=MESH
        )
        return carry

    lax.fori_loop(1, samp_count, greet, 0)

    perm_rows[...] = perm[...] - samp * runs
    stride = 2 * LANES
    for begin in range(0, runs, stride):
        columns = slice(begin, begin + stride)
        parts = pieces(
            jnp.concatenate(
                [
                    loads[:, columns],
                    coords[:, columns] * (1.0 / SUPPORT),
                    jnp.zeros((8 - coords.shape[0], stride), F32),
                ],
                axis=0,
            )
        )
        source[:, columns] = jnp.concatenate(parts[:2], axis=0).astype(BF16)
    depth = runs // 6
    for begin in range(0, depth, LANES):
        position[begin : begin + LANES, :] = (
            lax.broadcasted_iota(jnp.int32, (LANES, stride), 0) + begin
        )

    def sort_step(pair, carry):
        columns = pl.ds(pl.multiple_of(pair * stride, stride), stride)
        target = perm_rows[:, columns]
        total = jnp.zeros((2 * (rows + 8), stride), F32)
        for part in range(6):
            chosen = jnp.where(position[...] == target - part * depth, 1.0, 0.0).astype(BF16)
            total = total + jnp.dot(
                source[:, part * depth : (part + 1) * depth],
                chosen,
                preferred_element_type=F32,
            )
        result = total[0 : rows + 8] + total[rows + 8 :]
        sorted_loads[:, columns] = result[0:rows]
        coords_ext[:, pl.ds(pl.multiple_of(halo + pair * stride, LANES), stride)] = result[rows:]
        return carry

    def column_step(tile, carry):
        index = perm_rows[:, lane_tile(tile)].astype(F32)
        perm_column[lane_tile(tile), :] = jnp.broadcast_to(index, (LANES, LANES)).T
        return carry

    lane_id = lax.broadcasted_iota(jnp.int32, (1, LANES), 1).astype(F32)

    def unsort_begin(block_sums):
        for begin in range(0, runs, stride):
            columns = slice(begin, begin + stride)
            high, middle, _ = pieces(block_sums[:, columns])
            spread[:, columns] = jnp.concatenate([high, middle], axis=0).astype(BF16)

    def unsort(target, begin, end):
        def unsort_step(pair, carry):
            columns = pl.ds(pl.multiple_of(pair * stride, stride), stride)
            low_lanes = lane_id + (pair * stride).astype(F32)
            total = jnp.zeros((2 * rows, stride), F32)
            for part in range(6):
                index = perm_column[part * depth : (part + 1) * depth, :]
                chosen = jnp.concatenate(
                    [
                        jnp.where(index == low_lanes, 1.0, 0.0).astype(BF16),
                        jnp.where(index == low_lanes + float(LANES), 1.0, 0.0).astype(BF16),
                    ],
                    axis=1,
                )
                total = total + jnp.dot(
                    spread[:, part * depth : (part + 1) * depth],
                    chosen,
                    preferred_element_type=F32,
                )
            target[:, columns] = total[0:rows] + total[rows:]
            return carry

        lax.fori_loop(begin, end, unsort_step, 0)


    @pl.when(samp == 0)
    def _():
        coords_ext[:, 0:halo] = jnp.zeros((8, halo), F32)
        for turn in range(2):
            values[turn][0:edge] = jnp.zeros((edge, rows, LANES), BF16)

    @pl.when(samp == samp_count - 1)
    def _():
        coords_ext[:, extent - halo : extent] = jnp.zeros((8, halo), F32)
        for turn in range(2):
            values[turn][widened - edge : widened] = jnp.zeros((edge, rows, LANES), BF16)

    factors[chan] = factor[...]
    pl.semaphore_wait(barrier, 3 + samp_count - 1)

    per_chunk = blocks // CHUNKS
    below = (samp + samp_count - 1) % samp_count
    above = (samp + 1) % samp_count

    def halo_copy(source_ref, target_ref, turn, side, part):
        return pltpu.make_async_remote_copy(
            src_ref=source_ref,
            dst_ref=target_ref,
            send_sem=halo_send.at[turn, side, part],
            recv_sem=halo_recv.at[turn, side, part],
            device_id={"samp": below if side == 0 else above},
            device_id_type=MESH,
        )

    def halo_start(copies):
        for side, group in enumerate(copies):
            if group:
                @pl.when((samp > 0) if side == 0 else (samp < samp_count - 1))
                def _():
                    for copy in group:
                        copy.start()

    def halo_wait(copies):
        @pl.when(samp > 0)
        def _():
            for copy in copies[0]:
                copy.wait_send()
            for copy in copies[1]:
                copy.wait_recv()

        @pl.when(samp < samp_count - 1)
        def _():
            for copy in copies[1]:
                copy.wait_send()
            for copy in copies[0]:
                copy.wait_recv()

    def value_copies(turn, part):
        buffer = values[turn]
        begin, end = part * per_chunk, (part + 1) * per_chunk
        result = ([], [])
        if begin < edge:
            count = min(end, edge) - begin
            result[0].append(
                halo_copy(
                    buffer.at[pl.ds(edge + begin, count)],
                    buffer.at[pl.ds(edge + blocks + begin, count)],
                    turn + 1, 0, part,
                )
            )
        if end > blocks - edge:
            first = max(begin, blocks - edge)
            result[1].append(
                halo_copy(
                    buffer.at[pl.ds(edge + first, end - first)],
                    buffer.at[pl.ds(edge + first - blocks, end - first)],
                    turn + 1, 1, part,
                )
            )
        return result

    factor_copies = []
    for relation, peer in enumerate(chan_peers):
        factor_copies.append(
            pltpu.make_async_remote_copy(
                src_ref=factors.at[chan],
                dst_ref=factors.at[chan],
                send_sem=fac_send.at[relation],
                recv_sem=fac_recv.at[relation],
                device_id={"chan": peer},
                device_id_type=MESH,
            )
        )
        factor_copies[-1].start()

    def gather_copy(turn, kind, part, owner, peer):
        place = gathered.at[turn, owner, :, pl.ds(part * chunk, chunk)]
        return pltpu.make_async_remote_copy(
            src_ref=place,
            dst_ref=place,
            send_sem=gat_send.at[turn, kind, part],
            recv_sem=gat_recv.at[turn, kind, part],
            device_id={"chan": peer},
            device_id_type=MESH,
        )

    def gather_start(turn, part):
        gather_copy(turn, 1, part, chan, far_peer).start()
        gather_copy(turn, 0, part, chan, core_peer).start()

    def gather_forward(turn, part):
        gather_copy(turn, 1, part, far_peer, far_peer).wait_recv()
        gather_copy(turn, 2, part, far_peer, core_peer).start()

    def gather_finish(turn, part):
        gather_copy(turn, 0, part, chan, core_peer).wait_send()
        gather_copy(turn, 1, part, chan, far_peer).wait_send()
        gather_copy(turn, 2, part, far_peer, core_peer).wait_send()
        gather_copy(turn, 0, part, core_peer, core_peer).wait_recv()
        gather_copy(turn, 2, part, 3 - chan, core_peer).wait_recv()

    pairs = runs // stride // CHUNKS
    for part in range(CHUNKS):
        lax.fori_loop(part * pairs, (part + 1) * pairs, sort_step, 0)
        columns = pl.ds(part * chunk, chunk)
        gathered[0, chan, :, columns] = sorted_loads[:, columns].astype(BF16)
        gather_start(0, part)

    coord_copies = (
        [halo_copy(
            coords_ext.at[:, pl.ds(halo, halo)],
            coords_ext.at[:, pl.ds(extent - halo, halo)],
            0, 0, 0,
        )],
        [halo_copy(
            coords_ext.at[:, pl.ds(runs, halo)], coords_ext.at[:, pl.ds(0, halo)], 0, 1, 0
        )],
    )
    halo_start(coord_copies)

    row_id = lax.broadcasted_iota(jnp.int32, (8, LANES), 0)

    def own_step(tile, carry):
        point = coords_ext[:, lane_tile(tile + edge)]
        norm = jnp.sum(point * point, axis=0, keepdims=True)
        terms = jnp.where(row_id == 6, 1.0, jnp.where(row_id == 7, norm, -2.0 * point))
        high, middle, low = pieces(terms)
        stacked = jnp.concatenate(
            [high, middle, high, middle, low, high, jnp.zeros((LANES - 48, LANES), F32)], axis=0
        )
        own_terms[:, lane_tile(tile)] = stacked.astype(BF16)
        return carry

    lax.fori_loop(0, blocks, own_step, 0)

    def ext_step(tile, carry):
        point = coords_ext[:, lane_tile(tile)]
        norm = jnp.sum(point * point, axis=0, keepdims=True)
        terms = jnp.where(row_id == 6, norm, jnp.where(row_id == 7, 1.0, point))
        high, middle, low = pieces(terms)
        stacked = jnp.concatenate(
            [high, high, middle, middle, high, low, jnp.zeros((LANES - 48, LANES), F32)], axis=0
        )
        ext_terms[tile] = stacked.T.astype(BF16)
        return carry

    lax.fori_loop(edge, edge + blocks, ext_step, 0)
    lax.fori_loop(0, blocks, column_step, 0)
    for copy in factor_copies:
        copy.wait()
    coreg_rows = lax.dot_general(
        factor[...],
        factors[...].reshape(4 * rows, factor.shape[1]),
        (((1,), (1,)), ((), ())),
        precision=lax.Precision.HIGHEST,
        preferred_element_type=F32,
    )
    for number, piece in enumerate(pieces(coreg_rows)):
        coreg[number * rows : (number + 1) * rows, :] = piece.astype(BF16)
    halo_wait(coord_copies)
    lax.fori_loop(0, edge, ext_step, 0)
    lax.fori_loop(edge + blocks, widened, ext_step, 0)

    def window_start(block):
        return jnp.clip(nbrs[0, block] - samp * blocks + edge, 0, widened - slots)

    def tile_step(block, carry):
        start = window_start(block)
        count = jnp.full((1, LANES), counts[block], jnp.int32)
        own = own_terms[:, lane_tile(block)]
        for slot in range(slots):
            partner = ext_terms[start + slot]
            squared = jnp.dot(partner, own, preferred_element_type=F32)
            squared = jnp.maximum(squared, 1e-20)
            radius = squared * lax.rsqrt(squared)
            live = jnp.where(count > slot, 1.0, 0.0)
            remain = jnp.maximum(live - radius, 0.0)
            cubed = remain * remain * remain
            tile = cubed * cubed * (6.0 * radius + 1.0)
            tiles[block, slot * LANES : (slot + 1) * LANES, :] = tile.astype(BF16)
        return carry

    def mix(turn, part):
        gather_finish(turn, part)
        for begin in range(part * chunk, (part + 1) * chunk, stride):
            operand = gathered[turn, :, :, begin : begin + stride].reshape(4 * rows, stride)
            product = jnp.dot(coreg[...], operand, preferred_element_type=F32)
            mixed = product[0:rows] + product[rows : 2 * rows] + product[2 * rows : 3 * rows]
            for half in range(2):
                values[turn][edge + begin // LANES + half] = mixed[
                    :, half * LANES : (half + 1) * LANES
                ].astype(BF16)
        copies = value_copies(turn, part)
        halo_start(copies)
        return copies

    def merge(groups):
        return tuple([copy for group in groups for copy in group[side]] for side in range(2))

    diagonal = lax.broadcasted_iota(jnp.int32, (rows, rows), 0) == lax.broadcasted_iota(
        jnp.int32, (rows, rows), 1
    )
    noise_column = jnp.sum(jnp.where(diagonal, noise[...], 0.0), axis=1, keepdims=True)
    noise_wide = jnp.broadcast_to(noise_column, (rows, LANES))
    nothing = jnp.zeros((rows, LANES), F32)

    def apply_block(turn, block, operand):
        start = window_start(block)
        partner = jnp.concatenate([values[turn][start + slot] for slot in range(slots)], axis=1)
        summed = jnp.dot(partner, tiles[block], preferred_element_type=F32)
        return AMPLITUDE * summed + noise_wide * operand

    def reduce_chan_copy(turn, relation, owner, peer):
        return pltpu.make_async_remote_copy(
            src_ref=red_chan.at[turn, owner],
            dst_ref=red_chan.at[turn, owner],
            send_sem=rc_send.at[turn, relation],
            recv_sem=rc_recv.at[turn, relation],
            device_id={"chan": peer},
            device_id_type=MESH,
        )

    def reduce_begin(turn, parts):
        lines = []
        for part in parts:
            lines.append(jnp.sum(fold(part), axis=0, keepdims=True))
        lines.append(jnp.zeros((8 - len(parts), LANES), F32))
        red_chan[turn, chan] = jnp.concatenate(lines, axis=0)
        for relation, peer in enumerate(chan_peers):
            reduce_chan_copy(turn, relation, chan, peer).start()

    def reduce_samp_copy(turn, hop, owner):
        return pltpu.make_async_remote_copy(
            src_ref=red_samp.at[turn, owner],
            dst_ref=red_samp.at[turn, owner],
            send_sem=rs_send.at[turn, hop],
            recv_sem=rs_recv.at[turn, owner],
            device_id={"samp": (samp + hop) % samp_count},
            device_id_type=MESH,
        )

    def reduce_middle(turn):
        for relation, peer in enumerate(chan_peers):
            reduce_chan_copy(turn, relation, chan, peer).wait_send()
            reduce_chan_copy(turn, relation, peer, peer).wait_recv()
        total = red_chan[turn, 0] + red_chan[turn, 1] + red_chan[turn, 2] + red_chan[turn, 3]
        red_samp[turn, samp] = total

        def send(hop, carry):
            reduce_samp_copy(turn, hop, samp).start()
            return carry

        lax.fori_loop(1, samp_count, send, 0)

    def reduce_end(turn):
        def wait(hop, carry):
            reduce_samp_copy(turn, hop, samp).wait_send()
            reduce_samp_copy(turn, hop, (samp + hop) % samp_count).wait_recv()
            return carry

        lax.fori_loop(1, samp_count, wait, 0)

        def add(index, total):
            return total + red_samp[turn, index]

        total = lax.fori_loop(0, samp_count, add, jnp.zeros((8, LANES), F32))
        return [whole_sum(total[number : number + 1]) for number in range(3)]

    eighth = blocks // 8
    lax.fori_loop(0, eighth, tile_step, 0)
    gather_forward(0, 0)
    gather_forward(0, 1)
    lax.fori_loop(eighth, 2 * eighth, tile_step, 0)
    gather_forward(0, 2)
    gather_forward(0, 3)
    lax.fori_loop(2 * eighth, 3 * eighth, tile_step, 0)
    copies = [mix(0, 0), mix(0, 1), mix(0, 2), mix(0, 3)]
    lax.fori_loop(3 * eighth, blocks, tile_step, 0)
    halo_wait(merge(copies))

    def first_apply(block, carry):
        norm, dot, square = carry
        operand = sorted_loads[:, lane_tile(block)]
        mapped = apply_block(0, block, operand)
        image[:, lane_tile(block)] = mapped
        return norm + operand * operand, dot + operand * mapped, square + mapped * mapped

    sums = lax.fori_loop(0, blocks, first_apply, (nothing, nothing, nothing))
    reduce_begin(0, sums)
    unsort_begin(image)
    reduce_middle(0)
    unsort(image_out, 0, pairs)
    norm_now, dot, square = reduce_end(0)
    first_step = norm_now / dot
    norm_next = jnp.maximum(
        norm_now - 2.0 * first_step * dot + first_step * first_step * square, 0.0
    )
    ratio = norm_next / norm_now

    norm_sum = nothing
    for part in range(CHUNKS):
        for tile in range(part * per_chunk, (part + 1) * per_chunk):
            columns = slice(tile * LANES, (tile + 1) * LANES)
            operand = sorted_loads[:, columns]
            remainder = operand - first_step * image[:, columns]
            norm_sum = norm_sum + remainder * remainder
            step = remainder + ratio * operand
            direction[:, columns] = step
            gathered[1, chan, :, columns] = step.astype(BF16)
        gather_start(1, part)

    copies = []
    for part in range(CHUNKS):
        if part:
            unsort(image_out, part * pairs, (part + 1) * pairs)
        gather_forward(1, part)
        if part:
            copies.append(mix(1, part - 1))
    copies.append(mix(1, CHUNKS - 1))
    halo_wait(merge(copies))

    def second_apply(block, total):
        operand = direction[:, lane_tile(block)]
        mapped = apply_block(1, block, operand)
        image[:, lane_tile(block)] = mapped
        return total + operand * mapped

    dot_sum = lax.fori_loop(0, blocks, second_apply, nothing)
    reduce_begin(1, [norm_sum, dot_sum])
    unsort_begin(image)
    reduce_middle(1)
    unsort(second_out, 0, runs // stride)
    norm_last, dot_last, _ = reduce_end(1)
    second_step = norm_last / dot_last
    scalars[0:1, :] = jnp.broadcast_to(first_step, (1, LANES))
    scalars[1:2, :] = jnp.broadcast_to(ratio, (1, LANES))
    scalars[2:8, :] = jnp.broadcast_to(second_step, (6, LANES))


def finisher(loads, image, second_image, scalars, sol, res):
    first_step, ratio, second_step = (scalars[row : row + 1, 0:1] for row in range(3))
    right = loads[...]
    remainder = right - first_step * image[...]
    step = remainder + ratio * right
    sol[...] = first_step * right + second_step * step
    res[...] = remainder - second_step * second_image[...]


def per_device(loads, coords, coreg_factor, noise, run_perm, block_nbrs, nbr_count):
    rows, runs = loads.shape
    blocks, slots = block_nbrs.shape
    samp_count = lax.axis_size("samp")
    halo = (slots - 1) * LANES
    extent = runs + 2 * halo
    chans = lax.axis_size("chan")
    vmem = pl.BlockSpec(memory_space=pltpu.VMEM)
    smem = pl.BlockSpec(memory_space=pltpu.SMEM)
    wide = pltpu.VMEM((rows, runs), F32)
    wide_out = jax.ShapeDtypeStruct((rows, runs), F32)
    image, second_image, scalars = pl.pallas_call(
        functools.partial(solver, samp_count, blocks, slots),
        out_shape=[wide_out, wide_out, jax.ShapeDtypeStruct((8, LANES), F32)],
        in_specs=[vmem] * 5 + [smem] * 2,
        out_specs=[vmem] * 3,
        scratch_shapes=[
            pltpu.VMEM((2 * (rows + 8), runs), BF16),
            pltpu.VMEM((2 * rows, runs), BF16),
            wide,
            pltpu.VMEM((runs // 6, 2 * LANES), jnp.int32),
            pltpu.VMEM((1, runs), jnp.int32),
            pltpu.VMEM((runs, LANES), F32),
            pltpu.VMEM((8, extent), F32),
            pltpu.VMEM((LANES, runs), BF16),
            pltpu.VMEM((extent // LANES, LANES, LANES), BF16),
            pltpu.VMEM((blocks, slots * LANES, LANES), BF16),
            pltpu.VMEM((chans, rows, coreg_factor.shape[1]), F32),
            pltpu.VMEM((3 * rows, chans * rows), BF16),
            wide, wide,
            pltpu.VMEM((2, chans, rows, runs), BF16),
            pltpu.VMEM((extent // LANES, rows, LANES), BF16),
            pltpu.VMEM((extent // LANES, rows, LANES), BF16),
            pltpu.VMEM((2, chans, 8, LANES), F32),
            pltpu.VMEM((2, samp_count, 8, LANES), F32),
            pltpu.SemaphoreType.DMA((3,)),
            pltpu.SemaphoreType.DMA((3,)),
            pltpu.SemaphoreType.DMA((2, 3, CHUNKS)),
            pltpu.SemaphoreType.DMA((2, 3, CHUNKS)),
            pltpu.SemaphoreType.DMA((3, 2, CHUNKS)),
            pltpu.SemaphoreType.DMA((3, 2, CHUNKS)),
            pltpu.SemaphoreType.DMA((2, 3)),
            pltpu.SemaphoreType.DMA((2, 3)),
            pltpu.SemaphoreType.DMA((2, samp_count)),
            pltpu.SemaphoreType.DMA((2, samp_count)),
        ],
        compiler_params=pltpu.CompilerParams(
            collective_id=0, has_side_effects=True, vmem_limit_bytes=56 * 2**20
        ),
    )(
        loads,
        coords,
        coreg_factor,
        noise[None, :],
        run_perm[None, :],
        block_nbrs.T,
        nbr_count,
    )
    block = pl.BlockSpec((rows // 4, runs), lambda step: (step, 0))
    return pl.pallas_call(
        finisher,
        grid=(4,),
        out_shape=[wide_out, wide_out],
        in_specs=[block] * 3 + [pl.BlockSpec((8, LANES), lambda step: (0, 0))],
        out_specs=[block] * 2,
        compiler_params=pltpu.CompilerParams(vmem_limit_bytes=60 * 2**20),
    )(loads, image, second_image, scalars)


def solution(mesh):
    return jax.shard_map(
        per_device,
        mesh=mesh,
        in_specs=(
            P("chan", "samp"),
            P(None, "samp"),
            P("chan", None),
            P("chan"),
            P("samp"),
            P("samp", None),
            P("samp"),
        ),
        out_specs=(P("chan", "samp"), P("chan", "samp")),
        check_vma=False,
    )
```

```python
import functools

import jax
import jax.numpy as jnp
from jax import lax
from jax.experimental import pallas as pl
from jax.experimental.pallas import tpu as pltpu
from jax.sharding import PartitionSpec as P

SUPPORT = 5.0
AMPLITUDE = 0.05
LANES = 128
CHUNKS = 4
MESH = pl.DeviceIdType.MESH
F32 = jnp.float32
BF16 = jnp.bfloat16


def lane_tile(index):
    return pl.ds(pl.multiple_of(index * LANES, LANES), LANES)


def pieces(value):
    high = value.astype(BF16).astype(F32)
    rest = value - high
    middle = rest.astype(BF16).astype(F32)
    return high, middle, (rest - middle).astype(BF16).astype(F32)


def fold(value):
    total = value[0:8]
    for row in range(8, value.shape[0], 8):
        total = total + value[row : row + 8]
    return total


def whole_sum(value):
    return jnp.sum(jnp.sum(value, axis=0, keepdims=True), axis=1, keepdims=True)


def solver(
    samp_count, blocks, slots,
    loads, coords, factor, noise, perm, nbrs, counts,
    image_out, second_out, scalars,
    source, spread, sorted_loads, position, perm_rows, perm_column, coords_ext, own_terms, ext_terms, tiles,
    factors, coreg, direction, image, gathered, values_first, values_second,
    red_chan, red_samp,
    fac_send, fac_recv, gat_send, gat_recv, halo_send, halo_recv,
    rc_send, rc_recv, rs_send, rs_recv,
):
    rows, runs = loads.shape
    halo = (slots - 1) * LANES
    extent = runs + 2 * halo
    edge = slots - 1
    widened = blocks + 2 * edge
    values = (values_first, values_second)
    chunk = runs // CHUNKS
    samp = lax.axis_index("samp")
    chan = lax.axis_index("chan")
    core_peer = chan + 1 - 2 * (chan % 2)
    far_peer = (chan + 2) % 4
    chan_peers = (core_peer, far_peer, 3 - chan)

    barrier = pltpu.get_barrier_semaphore()
    for peer in chan_peers:
        pl.semaphore_signal(barrier, inc=1, device_id={"chan": peer}, device_id_type=MESH)

    def greet(hop, carry):
        pl.semaphore_signal(
            barrier, inc=1, device_id={"samp": (samp + hop) % samp_count}, device_id_type=MESH
        )
        return carry

    lax.fori_loop(1, samp_count, greet, 0)

    perm_rows[...] = perm[...] - samp * runs
    stride = 2 * LANES
    for begin in range(0, runs, stride):
        columns = slice(begin, begin + stride)
        parts = pieces(
            jnp.concatenate(
                [
                    loads[:, columns],
                    coords[:, columns] * (1.0 / SUPPORT),
                    jnp.zeros((8 - coords.shape[0], stride), F32),
                ],
                axis=0,
            )
        )
        source[:, columns] = jnp.concatenate(parts[:2], axis=0).astype(BF16)
    depth = runs // 6
    for begin in range(0, depth, LANES):
        position[begin : begin + LANES, :] = (
            lax.broadcasted_iota(jnp.int32, (LANES, stride), 0) + begin
        )

    def sort_step(pair, carry):
        columns = pl.ds(pl.multiple_of(pair * stride, stride), stride)
        target = perm_rows[:, columns]
        total = jnp.zeros((2 * (rows + 8), stride), F32)
        for part in range(6):
            chosen = jnp.where(position[...] == target - part * depth, 1.0, 0.0).astype(BF16)
            total = total + jnp.dot(
                source[:, part * depth : (part + 1) * depth],
                chosen,
                preferred_element_type=F32,
            )
        result = total[0 : rows + 8] + total[rows + 8 :]
        sorted_loads[:, columns] = result[0:rows]
        coords_ext[:, pl.ds(pl.multiple_of(halo + pair * stride, LANES), stride)] = result[rows:]
        return carry

    def column_step(tile, carry):
        index = perm_rows[:, lane_tile(tile)].astype(F32)
        perm_column[lane_tile(tile), :] = jnp.broadcast_to(index, (LANES, LANES)).T
        return carry

    lane_id = lax.broadcasted_iota(jnp.int32, (1, LANES), 1).astype(F32)

    def unsort_begin(block_sums):
        for begin in range(0, runs, stride):
            columns = slice(begin, begin + stride)
            high, middle, _ = pieces(block_sums[:, columns])
            spread[:, columns] = jnp.concatenate([high, middle], axis=0).astype(BF16)

    def unsort(target, begin, end):
        def unsort_step(pair, carry):
            columns = pl.ds(pl.multiple_of(pair * stride, stride), stride)
            low_lanes = lane_id + (pair * stride).astype(F32)
            total = jnp.zeros((2 * rows, stride), F32)
            for part in range(6):
                index = perm_column[part * depth : (part + 1) * depth, :]
                chosen = jnp.concatenate(
                    [
                        jnp.where(index == low_lanes, 1.0, 0.0).astype(BF16),
                        jnp.where(index == low_lanes + float(LANES), 1.0, 0.0).astype(BF16),
                    ],
                    axis=1,
                )
                total = total + jnp.dot(
                    spread[:, part * depth : (part + 1) * depth],
                    chosen,
                    preferred_element_type=F32,
                )
            target[:, columns] = total[0:rows] + total[rows:]
            return carry

        lax.fori_loop(begin, end, unsort_step, 0)


    @pl.when(samp == 0)
    def _():
        coords_ext[:, 0:halo] = jnp.zeros((8, halo), F32)
        for turn in range(2):
            values[turn][0:edge] = jnp.zeros((edge, rows, LANES), BF16)

    @pl.when(samp == samp_count - 1)
    def _():
        coords_ext[:, extent - halo : extent] = jnp.zeros((8, halo), F32)
        for turn in range(2):
            values[turn][widened - edge : widened] = jnp.zeros((edge, rows, LANES), BF16)

    factors[chan] = factor[...]
    pl.semaphore_wait(barrier, 3 + samp_count - 1)

    per_chunk = blocks // CHUNKS
    below = (samp + samp_count - 1) % samp_count
    above = (samp + 1) % samp_count

    def halo_copy(source_ref, target_ref, turn, side, part):
        return pltpu.make_async_remote_copy(
            src_ref=source_ref,
            dst_ref=target_ref,
            send_sem=halo_send.at[turn, side, part],
            recv_sem=halo_recv.at[turn, side, part],
            device_id={"samp": below if side == 0 else above},
            device_id_type=MESH,
        )

    def halo_start(copies):
        for side, group in enumerate(copies):
            if group:
                @pl.when((samp > 0) if side == 0 else (samp < samp_count - 1))
                def _():
                    for copy in group:
                        copy.start()

    def halo_wait(copies):
        @pl.when(samp > 0)
        def _():
            for copy in copies[0]:
                copy.wait_send()
            for copy in copies[1]:
                copy.wait_recv()

        @pl.when(samp < samp_count - 1)
        def _():
            for copy in copies[1]:
                copy.wait_send()
            for copy in copies[0]:
                copy.wait_recv()

    def value_copies(turn, part):
        buffer = values[turn]
        begin, end = part * per_chunk, (part + 1) * per_chunk
        result = ([], [])
        if begin < edge:
            count = min(end, edge) - begin
            result[0].append(
                halo_copy(
                    buffer.at[pl.ds(edge + begin, count)],
                    buffer.at[pl.ds(edge + blocks + begin, count)],
                    turn + 1, 0, part,
                )
            )
        if end > blocks - edge:
            first = max(begin, blocks - edge)
            result[1].append(
                halo_copy(
                    buffer.at[pl.ds(edge + first, end - first)],
                    buffer.at[pl.ds(edge + first - blocks, end - first)],
                    turn + 1, 1, part,
                )
            )
        return result

    factor_copies = []
    for relation, peer in enumerate(chan_peers):
        factor_copies.append(
            pltpu.make_async_remote_copy(
                src_ref=factors.at[chan],
                dst_ref=factors.at[chan],
                send_sem=fac_send.at[relation],
                recv_sem=fac_recv.at[relation],
                device_id={"chan": peer},
                device_id_type=MESH,
            )
        )
        factor_copies[-1].start()

    def gather_copy(turn, kind, part, owner, peer):
        place = gathered.at[turn, owner, :, pl.ds(part * chunk, chunk)]
        return pltpu.make_async_remote_copy(
            src_ref=place,
            dst_ref=place,
            send_sem=gat_send.at[turn, kind, part],
            recv_sem=gat_recv.at[turn, kind, part],
            device_id={"chan": peer},
            device_id_type=MESH,
        )

    def gather_start(turn, part):
        gather_copy(turn, 1, part, chan, far_peer).start()
        gather_copy(turn, 0, part, chan, core_peer).start()

    def gather_forward(turn, part):
        gather_copy(turn, 1, part, far_peer, far_peer).wait_recv()
        gather_copy(turn, 2, part, far_peer, core_peer).start()

    def gather_finish(turn, part):
        gather_copy(turn, 0, part, chan, core_peer).wait_send()
        gather_copy(turn, 1, part, chan, far_peer).wait_send()
        gather_copy(turn, 2, part, far_peer, core_peer).wait_send()
        gather_copy(turn, 0, part, core_peer, core_peer).wait_recv()
        gather_copy(turn, 2, part, 3 - chan, core_peer).wait_recv()

    pairs = runs // stride // CHUNKS
    for part in range(CHUNKS):
        lax.fori_loop(part * pairs, (part + 1) * pairs, sort_step, 0)
        columns = pl.ds(part * chunk, chunk)
        gathered[0, chan, :, columns] = sorted_loads[:, columns].astype(BF16)
        gather_start(0, part)

    coord_copies = (
        [halo_copy(
            coords_ext.at[:, pl.ds(halo, halo)],
            coords_ext.at[:, pl.ds(extent - halo, halo)],
            0, 0, 0,
        )],
        [halo_copy(
            coords_ext.at[:, pl.ds(runs, halo)], coords_ext.at[:, pl.ds(0, halo)], 0, 1, 0
        )],
    )
    halo_start(coord_copies)

    row_id = lax.broadcasted_iota(jnp.int32, (8, LANES), 0)

    def own_step(tile, carry):
        point = coords_ext[:, lane_tile(tile + edge)]
        norm = jnp.sum(point * point, axis=0, keepdims=True)
        terms = jnp.where(row_id == 6, 1.0, jnp.where(row_id == 7, norm, -2.0 * point))
        high, middle, low = pieces(terms)
        stacked = jnp.concatenate(
            [high, middle, high, middle, low, high, jnp.zeros((LANES - 48, LANES), F32)], axis=0
        )
        own_terms[:, lane_tile(tile)] = stacked.astype(BF16)
        return carry

    lax.fori_loop(0, blocks, own_step, 0)

    def ext_step(tile, carry):
        point = coords_ext[:, lane_tile(tile)]
        norm = jnp.sum(point * point, axis=0, keepdims=True)
        terms = jnp.where(row_id == 6, norm, jnp.where(row_id == 7, 1.0, point))
        high, middle, low = pieces(terms)
        stacked = jnp.concatenate(
            [high, high, middle, middle, high, low, jnp.zeros((LANES - 48, LANES), F32)], axis=0
        )
        ext_terms[tile] = stacked.T.astype(BF16)
        return carry

    lax.fori_loop(edge, edge + blocks, ext_step, 0)
    lax.fori_loop(0, blocks, column_step, 0)
    for copy in factor_copies:
        copy.wait()
    coreg_rows = lax.dot_general(
        factor[...],
        factors[...].reshape(4 * rows, factor.shape[1]),
        (((1,), (1,)), ((), ())),
        precision=lax.Precision.HIGHEST,
        preferred_element_type=F32,
    )
    for number, piece in enumerate(pieces(coreg_rows)):
        coreg[number * rows : (number + 1) * rows, :] = piece.astype(BF16)
    halo_wait(coord_copies)
    lax.fori_loop(0, edge, ext_step, 0)
    lax.fori_loop(edge + blocks, widened, ext_step, 0)

    def window_start(block):
        return jnp.clip(nbrs[0, block] - samp * blocks + edge, 0, widened - slots)

    def tile_step(block, carry):
        start = window_start(block)
        count = jnp.full((1, LANES), counts[block], jnp.int32)
        own = own_terms[:, lane_tile(block)]
        for slot in range(slots):
            partner = ext_terms[start + slot]
            squared = jnp.dot(partner, own, preferred_element_type=F32)
            squared = jnp.maximum(squared, 1e-20)
            radius = squared * lax.rsqrt(squared)
            live = jnp.where(count > slot, 1.0, 0.0)
            remain = jnp.maximum(live - radius, 0.0)
            cubed = remain * remain * remain
            tile = cubed * cubed * (6.0 * radius + 1.0)
            tiles[block, slot * LANES : (slot + 1) * LANES, :] = tile.astype(BF16)
        return carry

    def mix(turn, part):
        gather_finish(turn, part)
        for begin in range(part * chunk, (part + 1) * chunk, stride):
            operand = gathered[turn, :, :, begin : begin + stride].reshape(4 * rows, stride)
            product = jnp.dot(coreg[...], operand, preferred_element_type=F32)
            mixed = product[0:rows] + product[rows : 2 * rows] + product[2 * rows : 3 * rows]
            for half in range(2):
                values[turn][edge + begin // LANES + half] = mixed[
                    :, half * LANES : (half + 1) * LANES
                ].astype(BF16)
        copies = value_copies(turn, part)
        halo_start(copies)
        return copies

    def merge(groups):
        return tuple([copy for group in groups for copy in group[side]] for side in range(2))

    diagonal = lax.broadcasted_iota(jnp.int32, (rows, rows), 0) == lax.broadcasted_iota(
        jnp.int32, (rows, rows), 1
    )
    noise_column = jnp.sum(jnp.where(diagonal, noise[...], 0.0), axis=1, keepdims=True)
    noise_wide = jnp.broadcast_to(noise_column, (rows, LANES))
    nothing = jnp.zeros((rows, LANES), F32)

    def apply_block(turn, block, operand):
        start = window_start(block)
        partner = jnp.concatenate([values[turn][start + slot] for slot in range(slots)], axis=1)
        summed = jnp.dot(partner, tiles[block], preferred_element_type=F32)
        return AMPLITUDE * summed + noise_wide * operand

    def reduce_chan_copy(turn, relation, owner, peer):
        return pltpu.make_async_remote_copy(
            src_ref=red_chan.at[turn, owner],
            dst_ref=red_chan.at[turn, owner],
            send_sem=rc_send.at[turn, relation],
            recv_sem=rc_recv.at[turn, relation],
            device_id={"chan": peer},
            device_id_type=MESH,
        )

    def reduce_begin(turn, parts):
        lines = []
        for part in parts:
            lines.append(jnp.sum(fold(part), axis=0, keepdims=True))
        lines.append(jnp.zeros((8 - len(parts), LANES), F32))
        red_chan[turn, chan] = jnp.concatenate(lines, axis=0)
        for relation, peer in enumerate(chan_peers):
            reduce_chan_copy(turn, relation, chan, peer).start()

    def reduce_samp_copy(turn, hop, owner):
        return pltpu.make_async_remote_copy(
            src_ref=red_samp.at[turn, owner],
            dst_ref=red_samp.at[turn, owner],
            send_sem=rs_send.at[turn, hop],
            recv_sem=rs_recv.at[turn, owner],
            device_id={"samp": (samp + hop) % samp_count},
            device_id_type=MESH,
        )

    def reduce_middle(turn):
        for relation, peer in enumerate(chan_peers):
            reduce_chan_copy(turn, relation, chan, peer).wait_send()
            reduce_chan_copy(turn, relation, peer, peer).wait_recv()
        total = red_chan[turn, 0] + red_chan[turn, 1] + red_chan[turn, 2] + red_chan[turn, 3]
        red_samp[turn, samp] = total

        def send(hop, carry):
            reduce_samp_copy(turn, hop, samp).start()
            return carry

        lax.fori_loop(1, samp_count, send, 0)

    def reduce_end(turn):
        def wait(hop, carry):
            reduce_samp_copy(turn, hop, samp).wait_send()
            reduce_samp_copy(turn, hop, (samp + hop) % samp_count).wait_recv()
            return carry

        lax.fori_loop(1, samp_count, wait, 0)

        def add(index, total):
            return total + red_samp[turn, index]

        total = lax.fori_loop(0, samp_count, add, jnp.zeros((8, LANES), F32))
        return [whole_sum(total[number : number + 1]) for number in range(3)]

    eighth = blocks // 8
    lax.fori_loop(0, eighth, tile_step, 0)
    gather_forward(0, 0)
    gather_forward(0, 1)
    lax.fori_loop(eighth, 2 * eighth, tile_step, 0)
    gather_forward(0, 2)
    gather_forward(0, 3)
    lax.fori_loop(2 * eighth, 3 * eighth, tile_step, 0)
    copies = [mix(0, 0), mix(0, 1), mix(0, 2), mix(0, 3)]
    lax.fori_loop(3 * eighth, blocks, tile_step, 0)
    halo_wait(merge(copies))

    def first_apply(block, carry):
        norm, dot, square = carry
        operand = sorted_loads[:, lane_tile(block)]
        mapped = apply_block(0, block, operand)
        image[:, lane_tile(block)] = mapped
        return norm + operand * operand, dot + operand * mapped, square + mapped * mapped

    sums = lax.fori_loop(0, blocks, first_apply, (nothing, nothing, nothing), unroll=2)
    reduce_begin(0, sums)
    unsort_begin(image)
    reduce_middle(0)
    unsort(image_out, 0, pairs)
    norm_now, dot, square = reduce_end(0)
    first_step = norm_now / dot
    norm_next = jnp.maximum(
        norm_now - 2.0 * first_step * dot + first_step * first_step * square, 0.0
    )
    ratio = norm_next / norm_now

    norm_sum = nothing
    for part in range(CHUNKS):
        for tile in range(part * per_chunk, (part + 1) * per_chunk):
            columns = slice(tile * LANES, (tile + 1) * LANES)
            operand = sorted_loads[:, columns]
            remainder = operand - first_step * image[:, columns]
            norm_sum = norm_sum + remainder * remainder
            step = remainder + ratio * operand
            direction[:, columns] = step
            gathered[1, chan, :, columns] = step.astype(BF16)
        gather_start(1, part)

    copies = []
    for part in range(CHUNKS):
        if part:
            unsort(image_out, part * pairs, (part + 1) * pairs)
        gather_forward(1, part)
        if part:
            copies.append(mix(1, part - 1))
    copies.append(mix(1, CHUNKS - 1))
    halo_wait(merge(copies))

    def second_apply(block, total):
        operand = direction[:, lane_tile(block)]
        mapped = apply_block(1, block, operand)
        image[:, lane_tile(block)] = mapped
        return total + operand * mapped

    dot_sum = lax.fori_loop(0, blocks, second_apply, nothing, unroll=2)
    reduce_begin(1, [norm_sum, dot_sum])
    unsort_begin(image)
    reduce_middle(1)
    unsort(second_out, 0, runs // stride)
    norm_last, dot_last, _ = reduce_end(1)
    second_step = norm_last / dot_last
    scalars[0:1, :] = jnp.broadcast_to(first_step, (1, LANES))
    scalars[1:2, :] = jnp.broadcast_to(ratio, (1, LANES))
    scalars[2:8, :] = jnp.broadcast_to(second_step, (6, LANES))


def finisher(loads, image, second_image, scalars, sol, res):
    first_step, ratio, second_step = (scalars[row : row + 1, 0:1] for row in range(3))
    right = loads[...]
    remainder = right - first_step * image[...]
    step = remainder + ratio * right
    sol[...] = first_step * right + second_step * step
    res[...] = remainder - second_step * second_image[...]


def per_device(loads, coords, coreg_factor, noise, run_perm, block_nbrs, nbr_count):
    rows, runs = loads.shape
    blocks, slots = block_nbrs.shape
    samp_count = lax.axis_size("samp")
    halo = (slots - 1) * LANES
    extent = runs + 2 * halo
    chans = lax.axis_size("chan")
    vmem = pl.BlockSpec(memory_space=pltpu.VMEM)
    smem = pl.BlockSpec(memory_space=pltpu.SMEM)
    wide = pltpu.VMEM((rows, runs), F32)
    wide_out = jax.ShapeDtypeStruct((rows, runs), F32)
    image, second_image, scalars = pl.pallas_call(
        functools.partial(solver, samp_count, blocks, slots),
        out_shape=[wide_out, wide_out, jax.ShapeDtypeStruct((8, LANES), F32)],
        in_specs=[vmem] * 5 + [smem] * 2,
        out_specs=[vmem] * 3,
        scratch_shapes=[
            pltpu.VMEM((2 * (rows + 8), runs), BF16),
            pltpu.VMEM((2 * rows, runs), BF16),
            wide,
            pltpu.VMEM((runs // 6, 2 * LANES), jnp.int32),
            pltpu.VMEM((1, runs), jnp.int32),
            pltpu.VMEM((runs, LANES), F32),
            pltpu.VMEM((8, extent), F32),
            pltpu.VMEM((LANES, runs), BF16),
            pltpu.VMEM((extent // LANES, LANES, LANES), BF16),
            pltpu.VMEM((blocks, slots * LANES, LANES), BF16),
            pltpu.VMEM((chans, rows, coreg_factor.shape[1]), F32),
            pltpu.VMEM((3 * rows, chans * rows), BF16),
            wide, wide,
            pltpu.VMEM((2, chans, rows, runs), BF16),
            pltpu.VMEM((extent // LANES, rows, LANES), BF16),
            pltpu.VMEM((extent // LANES, rows, LANES), BF16),
            pltpu.VMEM((2, chans, 8, LANES), F32),
            pltpu.VMEM((2, samp_count, 8, LANES), F32),
            pltpu.SemaphoreType.DMA((3,)),
            pltpu.SemaphoreType.DMA((3,)),
            pltpu.SemaphoreType.DMA((2, 3, CHUNKS)),
            pltpu.SemaphoreType.DMA((2, 3, CHUNKS)),
            pltpu.SemaphoreType.DMA((3, 2, CHUNKS)),
            pltpu.SemaphoreType.DMA((3, 2, CHUNKS)),
            pltpu.SemaphoreType.DMA((2, 3)),
            pltpu.SemaphoreType.DMA((2, 3)),
            pltpu.SemaphoreType.DMA((2, samp_count)),
            pltpu.SemaphoreType.DMA((2, samp_count)),
        ],
        compiler_params=pltpu.CompilerParams(
            collective_id=0, has_side_effects=True, vmem_limit_bytes=56 * 2**20
        ),
    )(
        loads,
        coords,
        coreg_factor,
        noise[None, :],
        run_perm[None, :],
        block_nbrs.T,
        nbr_count,
    )
    block = pl.BlockSpec((rows // 4, runs), lambda step: (step, 0))
    return pl.pallas_call(
        finisher,
        grid=(4,),
        out_shape=[wide_out, wide_out],
        in_specs=[block] * 3 + [pl.BlockSpec((8, LANES), lambda step: (0, 0))],
        out_specs=[block] * 2,
        compiler_params=pltpu.CompilerParams(vmem_limit_bytes=60 * 2**20),
    )(loads, image, second_image, scalars)


def solution(mesh):
    return jax.shard_map(
        per_device,
        mesh=mesh,
        in_specs=(
            P("chan", "samp"),
            P(None, "samp"),
            P("chan", None),
            P("chan"),
            P("samp"),
            P("samp", None),
            P("samp"),
        ),
        out_specs=(P("chan", "samp"), P("chan", "samp")),
        check_vma=False,
    )
```

```python
import functools

import jax
import jax.numpy as jnp
from jax import lax
from jax.experimental import pallas as pl
from jax.experimental.pallas import tpu as pltpu
from jax.sharding import PartitionSpec as P

SUPPORT = 5.0
AMPLITUDE = 0.05
LANES = 128
CHUNKS = 4
MESH = pl.DeviceIdType.MESH
F32 = jnp.float32
BF16 = jnp.bfloat16


def lane_tile(index):
    return pl.ds(pl.multiple_of(index * LANES, LANES), LANES)


def pieces(value):
    high = value.astype(BF16).astype(F32)
    rest = value - high
    middle = rest.astype(BF16).astype(F32)
    return high, middle, (rest - middle).astype(BF16).astype(F32)


def fold(value):
    total = value[0:8]
    for row in range(8, value.shape[0], 8):
        total = total + value[row : row + 8]
    return total


def whole_sum(value):
    return jnp.sum(jnp.sum(value, axis=0, keepdims=True), axis=1, keepdims=True)


def solver(
    samp_count, blocks, slots,
    loads, coords, factor, noise, perm, nbrs, counts,
    image_out, second_out, scalars,
    source, spread, sorted_loads, position, perm_rows, perm_column, coords_ext, own_terms, ext_terms, tiles,
    factors, coreg, direction, image, gathered, values_first, values_second,
    red_chan, red_samp,
    fac_send, fac_recv, gat_send, gat_recv, halo_send, halo_recv,
    rc_send, rc_recv, rs_send, rs_recv,
):
    rows, runs = loads.shape
    halo = (slots - 1) * LANES
    extent = runs + 2 * halo
    edge = slots - 1
    widened = blocks + 2 * edge
    values = (values_first, values_second)
    chunk = runs // CHUNKS
    samp = lax.axis_index("samp")
    chan = lax.axis_index("chan")
    core_peer = chan + 1 - 2 * (chan % 2)
    far_peer = (chan + 2) % 4
    chan_peers = (core_peer, far_peer, 3 - chan)

    barrier = pltpu.get_barrier_semaphore()
    for peer in chan_peers:
        pl.semaphore_signal(barrier, inc=1, device_id={"chan": peer}, device_id_type=MESH)

    def greet(hop, carry):
        pl.semaphore_signal(
            barrier, inc=1, device_id={"samp": (samp + hop) % samp_count}, device_id_type=MESH
        )
        return carry

    lax.fori_loop(1, samp_count, greet, 0)

    perm_rows[...] = perm[...] - samp * runs
    stride = 2 * LANES
    for begin in range(0, runs, stride):
        columns = slice(begin, begin + stride)
        parts = pieces(
            jnp.concatenate(
                [
                    loads[:, columns],
                    coords[:, columns] * (1.0 / SUPPORT),
                    jnp.zeros((8 - coords.shape[0], stride), F32),
                ],
                axis=0,
            )
        )
        source[:, columns] = jnp.concatenate(parts[:2], axis=0).astype(BF16)
    depth = runs // 6
    for begin in range(0, depth, LANES):
        position[begin : begin + LANES, :] = (
            lax.broadcasted_iota(jnp.int32, (LANES, stride), 0) + begin
        )

    def sort_step(pair, carry):
        columns = pl.ds(pl.multiple_of(pair * stride, stride), stride)
        target = perm_rows[:, columns]
        total = jnp.zeros((2 * (rows + 8), stride), F32)
        for part in range(6):
            chosen = jnp.where(position[...] == target - part * depth, 1.0, 0.0).astype(BF16)
            total = total + jnp.dot(
                source[:, part * depth : (part + 1) * depth],
                chosen,
                preferred_element_type=F32,
            )
        result = total[0 : rows + 8] + total[rows + 8 :]
        sorted_loads[:, columns] = result[0:rows]
        coords_ext[:, pl.ds(pl.multiple_of(halo + pair * stride, LANES), stride)] = result[rows:]
        return carry

    def column_step(tile, carry):
        index = perm_rows[:, lane_tile(tile)].astype(F32)
        perm_column[lane_tile(tile), :] = jnp.broadcast_to(index, (LANES, LANES)).T
        return carry

    lane_id = lax.broadcasted_iota(jnp.int32, (1, LANES), 1).astype(F32)

    def unsort_begin(block_sums):
        for begin in range(0, runs, stride):
            columns = slice(begin, begin + stride)
            high, middle, _ = pieces(block_sums[:, columns])
            spread[:, columns] = jnp.concatenate([high, middle], axis=0).astype(BF16)

    def unsort(target, begin, end):
        def unsort_step(pair, carry):
            columns = pl.ds(pl.multiple_of(pair * stride, stride), stride)
            low_lanes = lane_id + (pair * stride).astype(F32)
            total = jnp.zeros((2 * rows, stride), F32)
            for part in range(6):
                index = perm_column[part * depth : (part + 1) * depth, :]
                chosen = jnp.concatenate(
                    [
                        jnp.where(index == low_lanes, 1.0, 0.0).astype(BF16),
                        jnp.where(index == low_lanes + float(LANES), 1.0, 0.0).astype(BF16),
                    ],
                    axis=1,
                )
                total = total + jnp.dot(
                    spread[:, part * depth : (part + 1) * depth],
                    chosen,
                    preferred_element_type=F32,
                )
            target[:, columns] = total[0:rows] + total[rows:]
            return carry

        lax.fori_loop(begin, end, unsort_step, 0)


    @pl.when(samp == 0)
    def _():
        coords_ext[:, 0:halo] = jnp.zeros((8, halo), F32)
        for turn in range(2):
            values[turn][0:edge] = jnp.zeros((edge, rows, LANES), BF16)

    @pl.when(samp == samp_count - 1)
    def _():
        coords_ext[:, extent - halo : extent] = jnp.zeros((8, halo), F32)
        for turn in range(2):
            values[turn][widened - edge : widened] = jnp.zeros((edge, rows, LANES), BF16)

    factors[chan] = factor[...]
    pl.semaphore_wait(barrier, 3 + samp_count - 1)

    per_chunk = blocks // CHUNKS
    below = (samp + samp_count - 1) % samp_count
    above = (samp + 1) % samp_count

    def halo_copy(source_ref, target_ref, turn, side, part):
        return pltpu.make_async_remote_copy(
            src_ref=source_ref,
            dst_ref=target_ref,
            send_sem=halo_send.at[turn, side, part],
            recv_sem=halo_recv.at[turn, side, part],
            device_id={"samp": below if side == 0 else above},
            device_id_type=MESH,
        )

    def halo_start(copies):
        for side, group in enumerate(copies):
            if group:
                @pl.when((samp > 0) if side == 0 else (samp < samp_count - 1))
                def _():
                    for copy in group:
                        copy.start()

    def halo_wait(copies):
        @pl.when(samp > 0)
        def _():
            for copy in copies[0]:
                copy.wait_send()
            for copy in copies[1]:
                copy.wait_recv()

        @pl.when(samp < samp_count - 1)
        def _():
            for copy in copies[1]:
                copy.wait_send()
            for copy in copies[0]:
                copy.wait_recv()

    def value_copies(turn, part):
        buffer = values[turn]
        begin, end = part * per_chunk, (part + 1) * per_chunk
        result = ([], [])
        if begin < edge:
            count = min(end, edge) - begin
            result[0].append(
                halo_copy(
                    buffer.at[pl.ds(edge + begin, count)],
                    buffer.at[pl.ds(edge + blocks + begin, count)],
                    turn + 1, 0, part,
                )
            )
        if end > blocks - edge:
            first = max(begin, blocks - edge)
            result[1].append(
                halo_copy(
                    buffer.at[pl.ds(edge + first, end - first)],
                    buffer.at[pl.ds(edge + first - blocks, end - first)],
                    turn + 1, 1, part,
                )
            )
        return result

    factor_copies = []
    for relation, peer in enumerate(chan_peers):
        factor_copies.append(
            pltpu.make_async_remote_copy(
                src_ref=factors.at[chan],
                dst_ref=factors.at[chan],
                send_sem=fac_send.at[relation],
                recv_sem=fac_recv.at[relation],
                device_id={"chan": peer},
                device_id_type=MESH,
            )
        )
        factor_copies[-1].start()

    def gather_copy(turn, kind, part, owner, peer):
        place = gathered.at[turn, owner, :, pl.ds(part * chunk, chunk)]
        return pltpu.make_async_remote_copy(
            src_ref=place,
            dst_ref=place,
            send_sem=gat_send.at[turn, kind, part],
            recv_sem=gat_recv.at[turn, kind, part],
            device_id={"chan": peer},
            device_id_type=MESH,
        )

    def gather_start(turn, part):
        gather_copy(turn, 1, part, chan, far_peer).start()
        gather_copy(turn, 0, part, chan, core_peer).start()

    def gather_forward(turn, part):
        gather_copy(turn, 1, part, far_peer, far_peer).wait_recv()
        gather_copy(turn, 2, part, far_peer, core_peer).start()

    def gather_finish(turn, part):
        gather_copy(turn, 0, part, chan, core_peer).wait_send()
        gather_copy(turn, 1, part, chan, far_peer).wait_send()
        gather_copy(turn, 2, part, far_peer, core_peer).wait_send()
        gather_copy(turn, 0, part, core_peer, core_peer).wait_recv()
        gather_copy(turn, 2, part, 3 - chan, core_peer).wait_recv()

    pairs = runs // stride // CHUNKS
    for part in range(CHUNKS):
        lax.fori_loop(part * pairs, (part + 1) * pairs, sort_step, 0)
        columns = pl.ds(part * chunk, chunk)
        gathered[0, chan, :, columns] = sorted_loads[:, columns].astype(BF16)
        gather_start(0, part)

    coord_copies = (
        [halo_copy(
            coords_ext.at[:, pl.ds(halo, halo)],
            coords_ext.at[:, pl.ds(extent - halo, halo)],
            0, 0, 0,
        )],
        [halo_copy(
            coords_ext.at[:, pl.ds(runs, halo)], coords_ext.at[:, pl.ds(0, halo)], 0, 1, 0
        )],
    )
    halo_start(coord_copies)

    row_id = lax.broadcasted_iota(jnp.int32, (8, LANES), 0)

    def own_step(tile, carry):
        point = coords_ext[:, lane_tile(tile + edge)]
        norm = jnp.sum(point * point, axis=0, keepdims=True)
        terms = jnp.where(row_id == 6, 1.0, jnp.where(row_id == 7, norm, -2.0 * point))
        high, middle, low = pieces(terms)
        stacked = jnp.concatenate(
            [high, middle, high, middle, low, high, jnp.zeros((LANES - 48, LANES), F32)], axis=0
        )
        own_terms[:, lane_tile(tile)] = stacked.astype(BF16)
        return carry

    lax.fori_loop(0, blocks, own_step, 0)

    def ext_step(tile, carry):
        point = coords_ext[:, lane_tile(tile)]
        norm = jnp.sum(point * point, axis=0, keepdims=True)
        terms = jnp.where(row_id == 6, norm, jnp.where(row_id == 7, 1.0, point))
        high, middle, low = pieces(terms)
        stacked = jnp.concatenate(
            [high, high, middle, middle, high, low, jnp.zeros((LANES - 48, LANES), F32)], axis=0
        )
        ext_terms[tile] = stacked.T.astype(BF16)
        return carry

    lax.fori_loop(edge, edge + blocks, ext_step, 0)
    lax.fori_loop(0, blocks, column_step, 0)
    for copy in factor_copies:
        copy.wait()
    coreg_rows = lax.dot_general(
        factor[...],
        factors[...].reshape(4 * rows, factor.shape[1]),
        (((1,), (1,)), ((), ())),
        precision=lax.Precision.HIGHEST,
        preferred_element_type=F32,
    )
    for number, piece in enumerate(pieces(coreg_rows)):
        coreg[number * rows : (number + 1) * rows, :] = piece.astype(BF16)
    halo_wait(coord_copies)
    lax.fori_loop(0, edge, ext_step, 0)
    lax.fori_loop(edge + blocks, widened, ext_step, 0)

    def window_start(block):
        return jnp.clip(nbrs[0, block] - samp * blocks + edge, 0, widened - slots)

    def tile_step(block, carry):
        start = window_start(block)
        count = jnp.full((1, LANES), counts[block], jnp.int32)
        own = own_terms[:, lane_tile(block)]
        for slot in range(slots):
            partner = ext_terms[start + slot]
            squared = jnp.dot(partner, own, preferred_element_type=F32)
            squared = jnp.maximum(squared, 1e-20)
            radius = squared * lax.rsqrt(squared)
            live = jnp.where(count > slot, 1.0, 0.0)
            remain = jnp.maximum(live - radius, 0.0)
            cubed = remain * remain * remain
            tile = cubed * cubed * (6.0 * radius + 1.0)
            tiles[block, slot * LANES : (slot + 1) * LANES, :] = tile.astype(BF16)
        return carry

    def mix(turn, part):
        gather_finish(turn, part)
        for begin in range(part * chunk, (part + 1) * chunk, stride):
            operand = gathered[turn, :, :, begin : begin + stride].reshape(4 * rows, stride)
            product = jnp.dot(coreg[...], operand, preferred_element_type=F32)
            mixed = product[0:rows] + product[rows : 2 * rows] + product[2 * rows : 3 * rows]
            for half in range(2):
                values[turn][edge + begin // LANES + half] = mixed[
                    :, half * LANES : (half + 1) * LANES
                ].astype(BF16)
        copies = value_copies(turn, part)
        halo_start(copies)
        return copies

    def merge(groups):
        return tuple([copy for group in groups for copy in group[side]] for side in range(2))

    diagonal = lax.broadcasted_iota(jnp.int32, (rows, rows), 0) == lax.broadcasted_iota(
        jnp.int32, (rows, rows), 1
    )
    noise_column = jnp.sum(jnp.where(diagonal, noise[...], 0.0), axis=1, keepdims=True)
    noise_wide = jnp.broadcast_to(noise_column, (rows, LANES))
    nothing = jnp.zeros((rows, LANES), F32)

    def apply_block(turn, block, operand):
        start = window_start(block)
        partner = jnp.concatenate([values[turn][start + slot] for slot in range(slots)], axis=1)
        summed = jnp.dot(partner, tiles[block], preferred_element_type=F32)
        return AMPLITUDE * summed + noise_wide * operand

    def reduce_chan_copy(turn, relation, owner, peer):
        return pltpu.make_async_remote_copy(
            src_ref=red_chan.at[turn, owner],
            dst_ref=red_chan.at[turn, owner],
            send_sem=rc_send.at[turn, relation],
            recv_sem=rc_recv.at[turn, relation],
            device_id={"chan": peer},
            device_id_type=MESH,
        )

    def reduce_begin(turn, parts):
        lines = []
        for part in parts:
            lines.append(jnp.sum(fold(part), axis=0, keepdims=True))
        lines.append(jnp.zeros((8 - len(parts), LANES), F32))
        red_chan[turn, chan] = jnp.concatenate(lines, axis=0)
        for relation, peer in enumerate(chan_peers):
            reduce_chan_copy(turn, relation, chan, peer).start()

    def reduce_samp_copy(turn, hop, owner):
        return pltpu.make_async_remote_copy(
            src_ref=red_samp.at[turn, owner],
            dst_ref=red_samp.at[turn, owner],
            send_sem=rs_send.at[turn, hop],
            recv_sem=rs_recv.at[turn, owner],
            device_id={"samp": (samp + hop) % samp_count},
            device_id_type=MESH,
        )

    def reduce_middle(turn):
        for relation, peer in enumerate(chan_peers):
            reduce_chan_copy(turn, relation, chan, peer).wait_send()
            reduce_chan_copy(turn, relation, peer, peer).wait_recv()
        total = red_chan[turn, 0] + red_chan[turn, 1] + red_chan[turn, 2] + red_chan[turn, 3]
        red_samp[turn, samp] = total

        def send(hop, carry):
            reduce_samp_copy(turn, hop, samp).start()
            return carry

        lax.fori_loop(1, samp_count, send, 0)

    def reduce_end(turn):
        def wait(hop, carry):
            reduce_samp_copy(turn, hop, samp).wait_send()
            reduce_samp_copy(turn, hop, (samp + hop) % samp_count).wait_recv()
            return carry

        lax.fori_loop(1, samp_count, wait, 0)

        def add(index, total):
            return total + red_samp[turn, index]

        total = lax.fori_loop(0, samp_count, add, jnp.zeros((8, LANES), F32))
        return [whole_sum(total[number : number + 1]) for number in range(3)]

    eighth = blocks // 8
    lax.fori_loop(0, eighth, tile_step, 0)
    gather_forward(0, 0)
    gather_forward(0, 1)
    lax.fori_loop(eighth, 2 * eighth, tile_step, 0)
    gather_forward(0, 2)
    gather_forward(0, 3)
    lax.fori_loop(2 * eighth, 3 * eighth, tile_step, 0)
    copies = [mix(0, 0), mix(0, 1), mix(0, 2), mix(0, 3)]
    lax.fori_loop(3 * eighth, blocks, tile_step, 0)
    halo_wait(merge(copies))

    def first_apply(block, carry):
        norm, dot, square = carry
        operand = sorted_loads[:, lane_tile(block)]
        mapped = apply_block(0, block, operand)
        image[:, lane_tile(block)] = mapped
        return norm + operand * operand, dot + operand * mapped, square + mapped * mapped

    sums = lax.fori_loop(0, blocks, first_apply, (nothing, nothing, nothing), unroll=4)
    reduce_begin(0, sums)
    unsort_begin(image)
    reduce_middle(0)
    unsort(image_out, 0, pairs)
    norm_now, dot, square = reduce_end(0)
    first_step = norm_now / dot
    norm_next = jnp.maximum(
        norm_now - 2.0 * first_step * dot + first_step * first_step * square, 0.0
    )
    ratio = norm_next / norm_now

    norm_sum = nothing
    for part in range(CHUNKS):
        for tile in range(part * per_chunk, (part + 1) * per_chunk):
            columns = slice(tile * LANES, (tile + 1) * LANES)
            operand = sorted_loads[:, columns]
            remainder = operand - first_step * image[:, columns]
            norm_sum = norm_sum + remainder * remainder
            step = remainder + ratio * operand
            direction[:, columns] = step
            gathered[1, chan, :, columns] = step.astype(BF16)
        gather_start(1, part)

    copies = []
    for part in range(CHUNKS):
        if part:
            unsort(image_out, part * pairs, (part + 1) * pairs)
        gather_forward(1, part)
        if part:
            copies.append(mix(1, part - 1))
    copies.append(mix(1, CHUNKS - 1))
    halo_wait(merge(copies))

    def second_apply(block, total):
        operand = direction[:, lane_tile(block)]
        mapped = apply_block(1, block, operand)
        image[:, lane_tile(block)] = mapped
        return total + operand * mapped

    dot_sum = lax.fori_loop(0, blocks, second_apply, nothing, unroll=4)
    reduce_begin(1, [norm_sum, dot_sum])
    unsort_begin(image)
    reduce_middle(1)
    unsort(second_out, 0, runs // stride)
    norm_last, dot_last, _ = reduce_end(1)
    second_step = norm_last / dot_last
    scalars[0:1, :] = jnp.broadcast_to(first_step, (1, LANES))
    scalars[1:2, :] = jnp.broadcast_to(ratio, (1, LANES))
    scalars[2:8, :] = jnp.broadcast_to(second_step, (6, LANES))


def finisher(loads, image, second_image, scalars, sol, res):
    first_step, ratio, second_step = (scalars[row : row + 1, 0:1] for row in range(3))
    right = loads[...]
    remainder = right - first_step * image[...]
    step = remainder + ratio * right
    sol[...] = first_step * right + second_step * step
    res[...] = remainder - second_step * second_image[...]


def per_device(loads, coords, coreg_factor, noise, run_perm, block_nbrs, nbr_count):
    rows, runs = loads.shape
    blocks, slots = block_nbrs.shape
    samp_count = lax.axis_size("samp")
    halo = (slots - 1) * LANES
    extent = runs + 2 * halo
    chans = lax.axis_size("chan")
    vmem = pl.BlockSpec(memory_space=pltpu.VMEM)
    smem = pl.BlockSpec(memory_space=pltpu.SMEM)
    wide = pltpu.VMEM((rows, runs), F32)
    wide_out = jax.ShapeDtypeStruct((rows, runs), F32)
    image, second_image, scalars = pl.pallas_call(
        functools.partial(solver, samp_count, blocks, slots),
        out_shape=[wide_out, wide_out, jax.ShapeDtypeStruct((8, LANES), F32)],
        in_specs=[vmem] * 5 + [smem] * 2,
        out_specs=[vmem] * 3,
        scratch_shapes=[
            pltpu.VMEM((2 * (rows + 8), runs), BF16),
            pltpu.VMEM((2 * rows, runs), BF16),
            wide,
            pltpu.VMEM((runs // 6, 2 * LANES), jnp.int32),
            pltpu.VMEM((1, runs), jnp.int32),
            pltpu.VMEM((runs, LANES), F32),
            pltpu.VMEM((8, extent), F32),
            pltpu.VMEM((LANES, runs), BF16),
            pltpu.VMEM((extent // LANES, LANES, LANES), BF16),
            pltpu.VMEM((blocks, slots * LANES, LANES), BF16),
            pltpu.VMEM((chans, rows, coreg_factor.shape[1]), F32),
            pltpu.VMEM((3 * rows, chans * rows), BF16),
            wide, wide,
            pltpu.VMEM((2, chans, rows, runs), BF16),
            pltpu.VMEM((extent // LANES, rows, LANES), BF16),
            pltpu.VMEM((extent // LANES, rows, LANES), BF16),
            pltpu.VMEM((2, chans, 8, LANES), F32),
            pltpu.VMEM((2, samp_count, 8, LANES), F32),
            pltpu.SemaphoreType.DMA((3,)),
            pltpu.SemaphoreType.DMA((3,)),
            pltpu.SemaphoreType.DMA((2, 3, CHUNKS)),
            pltpu.SemaphoreType.DMA((2, 3, CHUNKS)),
            pltpu.SemaphoreType.DMA((3, 2, CHUNKS)),
            pltpu.SemaphoreType.DMA((3, 2, CHUNKS)),
            pltpu.SemaphoreType.DMA((2, 3)),
            pltpu.SemaphoreType.DMA((2, 3)),
            pltpu.SemaphoreType.DMA((2, samp_count)),
            pltpu.SemaphoreType.DMA((2, samp_count)),
        ],
        compiler_params=pltpu.CompilerParams(
            collective_id=0, has_side_effects=True, vmem_limit_bytes=56 * 2**20
        ),
    )(
        loads,
        coords,
        coreg_factor,
        noise[None, :],
        run_perm[None, :],
        block_nbrs.T,
        nbr_count,
    )
    block = pl.BlockSpec((rows // 4, runs), lambda step: (step, 0))
    return pl.pallas_call(
        finisher,
        grid=(4,),
        out_shape=[wide_out, wide_out],
        in_specs=[block] * 3 + [pl.BlockSpec((8, LANES), lambda step: (0, 0))],
        out_specs=[block] * 2,
        compiler_params=pltpu.CompilerParams(vmem_limit_bytes=60 * 2**20),
    )(loads, image, second_image, scalars)


def solution(mesh):
    return jax.shard_map(
        per_device,
        mesh=mesh,
        in_specs=(
            P("chan", "samp"),
            P(None, "samp"),
            P("chan", None),
            P("chan"),
            P("samp"),
            P("samp", None),
            P("samp"),
        ),
        out_specs=(P("chan", "samp"), P("chan", "samp")),
        check_vma=False,
    )
```
